128 devices in a mesh: catalog: 16 (over y_lo, z, core), query: 4 (over x), dp: 2 (over y_hi).
Axes of the slice: x: 4, y: 4 (y_hi: 2, y_lo: 2; y = y_hi * 2 + y_lo), z: 4, core: 2. Of those that a mesh axis runs over, the one named last changes fastest.
Arguments:
- slab: bfloat16 [262144, 512], P('catalog'), may hold values from -6 to 6
- fetch_rows: int32 [16, 16, 512], P('catalog', None, ('query', 'dp')), may hold values from 0 to 16383, as said below
- w_in: bfloat16 [512, 2048], replicated, may hold values from -0.25 to 0.25
- b_in: float32 [2048], replicated, may hold values from -3 to 3
- w_out: bfloat16 [2048, 512], replicated, may hold values from -0.125 to 0.125
- query_emb: bfloat16 [8192, 512], P(('query', 'dp')), may hold values from -2400 to 2400
- item_counts: int32 [16, 16, 512], P('catalog'), may hold values from 1 to 199
- tile_blocks: int32 [64, 16, 8], P(('query', 'dp'), 'catalog'), may hold values from 0 to 63, as said below
- tile_count: int32 [64, 16], P(('query', 'dp'), 'catalog'), may hold values from 1 to 8
- pos_idx: int32 [8192], P(('query', 'dp')), may hold values from 0 to 131071, as said below
Outputs:
- cand_vectors: bfloat16 [16, 16, 512, 512], P('catalog', None, ('query', 'dp'))
- query_loss: float32 [8192], P(('query', 'dp'))
The draws below stay inside these ranges and needn't reach their ends.
Inputs may be any that keep to these rules, and one draw needn't show every extreme that they name: For each owner o the 8192 entries of fetch_rows[o] are distinct. The entries of tile_blocks[b, t] are distinct. `pos_idx`: each query's positive lies in a block listed for its query block.
All inputs are finite; a program needn't handle non-finite values.
Results may differ from the reference program's by a relative error of at most 0.005.
Values may be sent and summed in bfloat16 or wider, within the bound.
A program may use at most 192 MiB of HBM per device.

```python
import jax
import jax.numpy as jnp
from jax import lax

E = 512
H = 2048
BLOCK = 128
LIST = 8
SLOT = 512
U_DEV = 8192
ROWS_DEV = 16384
CATALOG_ROWS = 262144
QUERIES = 8192
QBLOCKS = 64
N_CATALOG = 16


def draw_fetch_rows(key, part):
    owner_keys = jax.random.split(key, N_CATALOG)

    def one_owner(owner_key):
        return jax.random.permutation(owner_key, ROWS_DEV)[:N_CATALOG * SLOT]
    return jax.vmap(one_owner)(owner_keys).reshape(N_CATALOG, N_CATALOG, SLOT).astype(jnp.int32)


def tile_plan(key):
    base_key = jax.random.fold_in(key, 7)
    heavy_key, count_key, full_key, block_key, pick_key = jax.random.split(base_key, 5)
    heavy_level = jax.random.randint(heavy_key, (N_CATALOG,), 0, 4)
    raw_counts = jax.random.randint(count_key, (QBLOCKS, N_CATALOG), 0, LIST)
    list_counts = 1 + raw_counts * (1 + heavy_level)[None, :] // 4
    full_device = jax.random.randint(full_key, (QBLOCKS,), 0, N_CATALOG)
    list_counts = jnp.where(jnp.arange(N_CATALOG)[None, :] == full_device[:, None], LIST, list_counts)
    block_keys = jax.random.split(block_key, QBLOCKS * N_CATALOG)
    list_blocks = jax.vmap(lambda one_key: jax.random.permutation(one_key, U_DEV // BLOCK)[:LIST])(block_keys)
    list_blocks = list_blocks.reshape(QBLOCKS, N_CATALOG, LIST)
    device_key, slot_key, row_key = jax.random.split(pick_key, 3)
    owner_device = jax.random.randint(device_key, (QUERIES,), 0, N_CATALOG)
    query_block = jnp.arange(QUERIES) // BLOCK
    count_here = list_counts[query_block, owner_device]
    list_slot = jax.random.randint(slot_key, (QUERIES,), 0, 1 << 20) % count_here
    chosen_block = list_blocks[query_block, owner_device, list_slot]
    row_offset = jax.random.randint(row_key, (QUERIES,), 0, BLOCK)
    positive = owner_device * U_DEV + chosen_block * BLOCK + row_offset
    return (list_blocks.astype(jnp.int32), list_counts.astype(jnp.int32), positive.astype(jnp.int32))


def draw_tile_blocks(key, part):
    return tile_plan(key)[0]


def draw_tile_count(key, part):
    return tile_plan(key)[1]


def draw_pos_idx(key, part):
    return tile_plan(key)[2]


def draw_query_emb(key, part):
    normal_key = jax.random.fold_in(key, 0)
    values = jnp.clip(jax.random.normal(normal_key, (QUERIES, E), jnp.float32), -6.0, 6.0)
    return values.astype(jnp.bfloat16)


def plant(values, rng, smallest, largest):
    spot = [jax.random.randint(jax.random.fold_in(rng, axis), (), 0, length) for axis, length in enumerate(values.shape)]
    widest = values.shape.index(max(values.shape))
    next_to = spot[:widest] + [(spot[widest] + 1) % values.shape[widest]] + spot[widest + 1:]
    return values.at[tuple(spot)].set(smallest).at[tuple(next_to)].set(largest)


def steps_of(stream_key, shape, cuts, low, largest):
    loudness, own = 1.0, jax.random.fold_in(stream_key, 6)
    for axis_at, shards_of in cuts:
        steps = jnp.exp(jax.random.uniform(jax.random.fold_in(own, axis_at), (shards_of,), jnp.float32, low / len(cuts), largest / len(cuts)))
        loudness = loudness * jnp.repeat(steps, shape[axis_at] // shards_of).reshape([-1 if axis == axis_at else 1 for axis in range(len(shape))])
    return loudness


def normal_values(stream_key, extent, width, bound, shards=(), held_as=jnp.bfloat16):
    array = width * jax.random.normal(stream_key, extent, jnp.float32)
    if shards:
        array = array * steps_of(stream_key, extent, shards, -0.22, 0.18)
    return jnp.clip(array, -bound, bound).astype(held_as)


def setup_inputs(seed: int = 0) -> dict:
    arg_keys = jax.random.split(jax.random.key(seed), 11)
    slab = normal_values(arg_keys[0], (CATALOG_ROWS, E), 1.0, 6.0, ((0, 16),))
    fetch_rows = draw_fetch_rows(jax.random.fold_in(arg_keys[10], 71), 0)
    w_in = normal_values(arg_keys[2], (E, H), E ** -0.5, 0.25)
    b_in = normal_values(arg_keys[3], (H,), 0.5, 3.0, (), jnp.float32)
    w_out = normal_values(arg_keys[4], (H, E), H ** -0.5, 0.125)
    query_emb = draw_query_emb(jax.random.fold_in(arg_keys[10], 71), 0)
    item_counts = plant(jax.random.randint(arg_keys[6], (N_CATALOG, N_CATALOG, SLOT), 1, 200), jax.random.fold_in(arg_keys[6], 1), 1, 199).astype(jnp.int32)
    tile_blocks = draw_tile_blocks(jax.random.fold_in(arg_keys[10], 71), 0)
    tile_count = draw_tile_count(jax.random.fold_in(arg_keys[10], 71), 0)
    pos_idx = draw_pos_idx(jax.random.fold_in(arg_keys[10], 71), 0)
    return {"slab": slab, "fetch_rows": fetch_rows, "w_in": w_in, "b_in": b_in, "w_out": w_out, "query_emb": query_emb, "item_counts": item_counts, "tile_blocks": tile_blocks, "tile_count": tile_count, "pos_idx": pos_idx}


def item_tower(item_rows, w_in, b_in, w_out):
    hidden = jnp.maximum(jnp.dot(item_rows, w_in, preferred_element_type=jnp.float32) + b_in, 0.0).astype(jnp.bfloat16)
    output = jnp.dot(hidden, w_out, preferred_element_type=jnp.float32)
    return (output * lax.rsqrt(lax.optimization_barrier(jnp.sum(output * output, axis=-1, keepdims=True)) + 1e-06)).astype(jnp.bfloat16)

def reference(slab, fetch_rows, w_in, b_in, w_out, query_emb, item_counts, tile_blocks, tile_count, pos_idx):
    owners = jnp.arange(N_CATALOG, dtype=jnp.int32)[:, None, None]
    fetched = jnp.take(slab, (owners * ROWS_DEV + fetch_rows).reshape(-1), axis=0).reshape(N_CATALOG, N_CATALOG, SLOT, E)
    arrived = jnp.transpose(fetched, (1, 0, 2, 3)).reshape(N_CATALOG, U_DEV, E)
    vectors = lax.map(lambda item_rows: item_tower(item_rows, w_in, b_in, w_out), arrived)
    cand_vectors = vectors.reshape(N_CATALOG, N_CATALOG, SLOT, E)
    log_counts = jnp.log(item_counts.astype(jnp.float32)).reshape(N_CATALOG, U_DEV // BLOCK, BLOCK)
    blocks = vectors.reshape(N_CATALOG, U_DEV // BLOCK, BLOCK, E)
    queries = query_emb.reshape(QBLOCKS, BLOCK, E)
    positives = pos_idx.reshape(QBLOCKS, BLOCK)
    devices = jnp.arange(N_CATALOG, dtype=jnp.int32)[:, None]
    offsets = jnp.arange(BLOCK, dtype=jnp.int32)[None, None, :]
    slots_list = jnp.arange(LIST, dtype=jnp.int32)[None, :]

    def one_block(inputs):
        query_rows, listed, counts, wanted = inputs
        chosen = blocks[devices, listed]
        scores = jnp.einsum('qe,tlce->qtlc', query_rows.astype(jnp.float32), chosen.astype(jnp.float32))
        scores = scores - log_counts[devices, listed][None]
        valid_mask = (slots_list < counts[:, None])[None, :, :, None]
        peak_score = lax.optimization_barrier(jnp.max(jnp.where(valid_mask, scores, -1e+30), axis=(1, 2, 3)))
        exp_total = lax.optimization_barrier(jnp.sum(jnp.where(valid_mask, jnp.exp(scores - peak_score[:, None, None, None]), 0.0), axis=(1, 2, 3)))
        column_ids = devices[:, :, None] * U_DEV + listed[:, :, None] * BLOCK + offsets
        match_mask = (column_ids[None] == wanted[:, None, None, None]) & valid_mask
        positive_score = lax.optimization_barrier(jnp.sum(jnp.where(match_mask, scores, 0.0), axis=(1, 2, 3)))
        return peak_score + jnp.log(exp_total) - positive_score
    query_loss = lax.map(one_block, (queries, tile_blocks, tile_count, positives)).reshape(QUERIES)
    return (cand_vectors, query_loss)
```

```python
import functools

import jax
import jax.numpy as jnp
from jax import lax
from jax.experimental import pallas as pl
from jax.experimental.pallas import tpu as pltpu
from jax.sharding import PartitionSpec as P

MESH = pl.DeviceIdType.MESH
ANY = pl.BlockSpec(memory_space=pl.ANY)
VMEM = pl.BlockSpec(memory_space=pltpu.VMEM)
SMEM = pl.BlockSpec(memory_space=pltpu.SMEM)

E = 512
H = 2048
NC = 16
NX = 4
ND = 2
NJ = NX * ND
SUB = 64
LIST = 8
ROWS = 16384
QROWS = 1024
QB = QROWS // 128
HALF = QROWS // 2
SLAB_CHUNK = 1024
JOBS = 4
LOW = -1e30


def flip(value, bits, width):
    out = value
    for bit in range(width):
        if (bits >> bit) & 1:
            out = out + (1 << bit) * (1 - 2 * ((value // (1 << bit)) % 2))
    return out


FLOWS = (
    ("y", (0, 0), 0, 256, None),
    ("r", (0, 0), 0, 256, None),
    ("l", (0, 0), 256, 256, None),
    ("y", (0, 0), 256, 256, None),
    ("r", (0, 0), 256, 256, None),
    ("l", (0, 0), 0, 256, None),
    ("r", (-1, 0), 0, 256, 1),
    ("l", (1, 0), 256, 256, 2),
    ("r", (0, 1), 0, 256, 0),
    ("l", (0, 1), 0, 256, 0),
    ("y", (1, 0), 256, 256, 2),
    ("y", (-1, 0), 256, 256, 4),
    ("y", (2, 0), 256, 256, 7),
    ("r", (-1, 1), 0, 128, 8),
    ("l", (1, 1), 128, 128, 9),
)


def landed(flow):
    hop, (ox, oy), *_ = FLOWS[flow]
    return {"r": (ox - 1, oy), "l": (ox + 1, oy), "y": (ox, 1 - oy)}[hop]


def tower_kernel(
    fetch, slab, query, pos, lists, counts, w_in, b_in, w_out,
    queries, meta_all, cand_out,
    chunk, table, rowbuf, staged, arrived, meta, w_in_v, w_out_v, cand,
    slab_sem, w_sem, own_sem, meta_send, meta_recv, a2a_send, a2a_recv, flow_send, flow_recv, core_send, core_recv, out_sem,
):
    t = lax.axis_index("catalog")
    x = lax.axis_index("query")
    d = lax.axis_index("dp")
    core = t % 2
    j = x * ND + d

    n_chunks = ROWS // SLAB_CHUNK
    depth = chunk.shape[0]

    def slab_copy(n):
        slot = n % depth
        rows = pl.ds(pl.multiple_of(n * SLAB_CHUNK, SLAB_CHUNK), SLAB_CHUNK)
        return pltpu.make_async_copy(slab.at[rows], chunk.at[slot], slab_sem.at[slot])

    for n in range(depth):
        slab_copy(n).start()

    meta_peers = [(dx, dd) for dx in range(NX) for dd in range(ND) if (dx, dd) != (0, 0)]
    right, left = (x + 1) % NX, (x + NX - 1) % NX
    hop_to = {
        "r": {"catalog": t, "query": right, "dp": d},
        "l": {"catalog": t, "query": left, "dp": d},
        "y": {"catalog": flip(t, 8, 4), "query": x, "dp": 1 - d},
    }
    sibling = {"catalog": flip(t, 1, 4), "query": x, "dp": d}

    barrier = pltpu.get_barrier_semaphore()
    n_peers = 0
    for k in range(1, NC):
        pl.semaphore_signal(barrier, inc=1, device_id={"catalog": flip(t, k, 4), "query": x, "dp": d}, device_id_type=MESH)
        n_peers += 1
    for dx, dd in meta_peers:
        pl.semaphore_signal(
            barrier, inc=1, device_id={"catalog": t, "query": (x + dx) % NX, "dp": (d + dd) % ND}, device_id_type=MESH
        )
        n_peers += 1
    pl.semaphore_signal(barrier, inc=1, device_id=hop_to["y"], device_id_type=MESH)
    n_peers += 1

    meta[...] = jnp.zeros_like(meta)
    meta[0:QB, :] = pos[...]
    meta[QB : 2 * QB, 0:LIST] = lists[:, 0, :]
    meta[QB : 2 * QB, LIST : LIST + 1] = counts[...]
    pl.semaphore_wait(barrier, n_peers)

    def origin(place):
        ox, oy = place
        xo = (x + ox + NX) % NX
        return xo * ND + (1 - d if oy else d)

    def flow_copy(n):
        hop, place, first, count, _ = FLOWS[n]
        jo = origin(place)
        rows = pl.ds(pl.multiple_of(core * HALF + first, 128), count)
        src = query.at[rows] if place == (0, 0) else queries.at[jo, rows]
        return pltpu.make_async_remote_copy(
            src_ref=src,
            dst_ref=queries.at[jo, rows],
            send_sem=flow_send.at[n],
            recv_sem=flow_recv.at[n],
            device_id=hop_to[hop],
            device_id_type=MESH,
        )

    def core_copy(n):
        _, _, first, count, _ = FLOWS[n]
        jo = origin(landed(n))
        rows = pl.ds(pl.multiple_of(core * HALF + first, 128), count)
        return pltpu.make_async_remote_copy(
            src_ref=queries.at[jo, rows],
            dst_ref=queries.at[jo, rows],
            send_sem=core_send.at[n],
            recv_sem=core_recv.at[n],
            device_id=sibling,
            device_id_type=MESH,
        )

    def advance(flows):
        for n in flows:
            flow_copy(n).wait_recv()
            for later, flow in enumerate(FLOWS):
                if flow[4] == n:
                    flow_copy(later).start()
            core_copy(n).start()

    for n, flow in enumerate(FLOWS):
        if flow[4] is None:
            flow_copy(n).start()

    def meta_copy(n):
        dx, dd = meta_peers[n]
        return pltpu.make_async_remote_copy(
            src_ref=meta,
            dst_ref=meta_all.at[j],
            send_sem=meta_send.at[n],
            recv_sem=meta_recv.at[n],
            device_id={"catalog": t, "query": (x + dx) % NX, "dp": (d + dd) % ND},
            device_id_type=MESH,
        )

    for n in range(len(meta_peers)):
        meta_copy(n).start()
    own_query = pltpu.make_async_copy(query, queries.at[j], own_sem.at[0])
    own_meta = pltpu.make_async_copy(meta, meta_all.at[j], own_sem.at[1])
    own_query.start()
    own_meta.start()

    @pl.loop(0, n_chunks)
    def _(n):
        slot = n % depth
        slab_copy(n).wait()

        @pl.loop(0, SLAB_CHUNK // 64)
        def _(i):
            rows = pl.ds(pl.multiple_of(i * 64, 64), 64)
            to = pl.ds(pl.multiple_of(n * SLAB_CHUNK + i * 64, 64), 64)
            table[to, :] = chunk[slot, rows, :].astype(jnp.float32)

        @pl.when(n + depth < n_chunks)
        def _():
            slab_copy(n + depth).start()

    w_in_copy = pltpu.make_async_copy(w_in, w_in_v, w_sem.at[0])
    w_out_copy = pltpu.make_async_copy(w_out, w_out_v, w_sem.at[1])
    w_in_copy.start()
    w_out_copy.start()

    def a2a_copy(k):
        to = flip(t, k, 4)
        return pltpu.make_async_remote_copy(
            src_ref=staged.at[k],
            dst_ref=arrived.at[t],
            send_sem=a2a_send.at[k],
            recv_sem=a2a_recv.at[k],
            device_id={"catalog": to, "query": x, "dp": d},
            device_id_type=MESH,
        )

    for k in range(NC - 1, -1, -1):
        to = flip(t, k, 4)

        @pl.loop(0, SUB // 16)
        def _(i):
            for u in range(16):
                row = fetch[0, to, i * 16 + u]
                rowbuf[pl.ds(i * 16 + u, 1), :] = table[pl.ds(row, 1), :]

        if k:
            staged[k] = rowbuf[...].astype(jnp.bfloat16)
            a2a_copy(k).start()
        else:
            arrived[t] = rowbuf[...].astype(jnp.bfloat16)

    advance((0, 1, 2))
    w_in_copy.wait()
    w_out_copy.wait()

    def tower(group):
        base = 4 * flip(t // 4, group, 2)
        for k in range(4 * group, 4 * group + 4):
            if k:
                a2a_copy(k).wait_recv()
        rows = arrived[pl.ds(base, 4)].reshape(4 * SUB, E)
        hidden = jnp.maximum(jnp.dot(rows, w_in_v[...], preferred_element_type=jnp.float32) + b_in[...], 0.0).astype(jnp.bfloat16)
        y = jnp.dot(hidden, w_out_v[...], preferred_element_type=jnp.float32)
        normed = y * lax.rsqrt(jnp.sum(y * y, axis=-1, keepdims=True) + 1e-06)
        cand[pl.ds(base, 4)] = normed.astype(jnp.bfloat16).reshape(4, SUB, E)
        pltpu.make_async_copy(cand.at[pl.ds(base, 4)], cand_out.at[pl.ds(base, 4)], out_sem.at[group]).start()

    tower(0)
    advance((3, 4, 5))
    tower(1)
    advance((7, 6, 8, 9))
    tower(2)
    tower(3)
    advance((10, 11, 12, 13, 14))

    for group in range(4):
        base = 4 * flip(t // 4, group, 2)
        pltpu.make_async_copy(cand.at[pl.ds(base, 4)], cand_out.at[pl.ds(base, 4)], out_sem.at[group]).wait()
    for k in range(1, NC):
        a2a_copy(k).wait_send()
    for n in range(len(FLOWS)):
        flow_copy(n).wait_send()
        core_copy(n).wait()
    for n in range(len(meta_peers)):
        meta_copy(n).wait()
    own_query.wait()
    own_meta.wait()


def run_tower(fetch, slab, query, pos, lists, counts, w_in, b_in, w_out):
    dma = pltpu.SemaphoreType.DMA
    return pl.pallas_call(
        tower_kernel,
        out_shape=(
            jax.ShapeDtypeStruct((NJ, QROWS, E), jnp.bfloat16),
            jax.ShapeDtypeStruct((NJ, 2 * QB, 128), jnp.int32),
            jax.ShapeDtypeStruct((NC, SUB, E), jnp.bfloat16),
        ),
        in_specs=[SMEM, ANY, ANY, VMEM, VMEM, VMEM, ANY, VMEM, ANY],
        out_specs=(ANY, ANY, ANY),
        scratch_shapes=[
            pltpu.VMEM((4, SLAB_CHUNK, E), jnp.bfloat16),
            pltpu.VMEM((ROWS, E), jnp.float32),
            pltpu.VMEM((SUB, E), jnp.float32),
            pltpu.VMEM((NC, SUB, E), jnp.bfloat16),
            pltpu.VMEM((NC, SUB, E), jnp.bfloat16),
            pltpu.VMEM((2 * QB, 128), jnp.int32),
            pltpu.VMEM((E, H), jnp.bfloat16),
            pltpu.VMEM((H, E), jnp.bfloat16),
            pltpu.VMEM((NC, SUB, E), jnp.bfloat16),
            dma((4,)),
            dma((2,)),
            dma((2,)),
            dma((NJ - 1,)),
            dma((NJ - 1,)),
            dma((NC,)),
            dma((NC,)),
            dma((len(FLOWS),)),
            dma((len(FLOWS),)),
            dma((len(FLOWS),)),
            dma((len(FLOWS),)),
            dma((4,)),
        ],
        compiler_params=pltpu.CompilerParams(
            collective_id=0, has_side_effects=True, vmem_limit_bytes=58 * 1024 * 1024
        ),
        cost_estimate=pl.CostEstimate(flops=4 * 1024 * E * H, bytes_accessed=32 << 20, transcendentals=0),
        name="tower",
    )(fetch, slab, query, pos, lists, counts, w_in, b_in, w_out)


def score_kernel(
    queries, meta_all, cand_in, item_counts,
    stats, cand_out,
    q, meta_s, meta_v, cand, logt, neg_log, jobs, top, total, positive,
    q_sem, sem,
):
    t = lax.axis_index("catalog")
    x = lax.axis_index("query")
    d = lax.axis_index("dp")
    j = x * ND + d

    to_smem = pltpu.make_async_copy(meta_all, meta_s, sem.at[0])
    to_vmem = pltpu.make_async_copy(meta_all, meta_v, sem.at[1])
    cand_load = pltpu.make_async_copy(cand_in, cand, sem.at[2])
    cand_store = pltpu.make_async_copy(cand, cand_out, sem.at[3])
    to_smem.start()
    to_vmem.start()
    cand_load.start()
    q_loads = [pltpu.make_async_copy(queries.at[n], q.at[pl.ds(n * QROWS, QROWS)], q_sem.at[n]) for n in range(NJ)]
    for load in q_loads:
        load.start()

    top[...] = jnp.full_like(top, LOW)
    total[...] = jnp.zeros_like(total)
    positive[...] = jnp.zeros_like(positive)
    logt[...] = jnp.transpose(-jnp.log(item_counts[...].astype(jnp.float32)))
    own = logt[pl.ds(pl.multiple_of(j * SUB, SUB), SUB), :]
    for o in range(NC):
        neg_log[o] = jnp.broadcast_to(own[:, o : o + 1], (SUB, 128))

    to_smem.wait()

    def list_block(b, n):
        count = meta_s[b // QB, QB + b % QB, LIST]
        for e in range(LIST):
            block = meta_s[b // QB, QB + b % QB, e]
            jobs[n] = b * NC + block // 4
            n = n + jnp.where((e < count) & (block % 4 == x), 1, 0)
        return n

    n_jobs = lax.fori_loop(0, NJ * QB, list_block, jnp.int32(0))
    for u in range(JOBS):
        jobs[n_jobs + u] = NJ * QB * NC
    to_vmem.wait()
    cand_load.wait()
    cand_store.start()
    for load in q_loads:
        load.wait()

    row_ids = lax.broadcasted_iota(jnp.int32, (SUB, 128), 0)

    @pl.loop(0, (n_jobs + JOBS - 1) // JOBS)
    def _(step):
        found = []
        for u in range(JOBS):
            job = jobs[step * JOBS + u]
            b, o = job // NC, job % NC
            b_q = jnp.minimum(b, NJ * QB - 1)
            block = q[pl.ds(pl.multiple_of(b_q * 128, 128), 128), :]
            scores = lax.dot_general(cand[o], block, (((1,), (1,)), ((), ())), preferred_element_type=jnp.float32)
            scores = scores + neg_log[o]
            wanted = meta_v[b_q // QB, pl.ds(b_q % QB, 1), :] - (t * (NC * 512) + o * 512 + j * SUB)
            peak = jnp.max(scores, axis=0, keepdims=True)
            mass = jnp.sum(jnp.exp(scores - peak), axis=0, keepdims=True)
            match = jnp.sum(jnp.where(row_ids == wanted, scores, 0.0), axis=0, keepdims=True)
            found.append((b, peak, mass, match))
        for b, peak, mass, match in found:
            at = pl.ds(b, 1)
            old = top[at, :]
            new = jnp.maximum(old, peak)
            total[at, :] = total[at, :] * jnp.exp(old - new) + mass * jnp.exp(peak - new)
            positive[at, :] = positive[at, :] + match
            top[at, :] = new

    for n in range(NJ):
        stats[n, 0:QB, :] = top[n * QB : (n + 1) * QB, :]
        stats[n, QB : 2 * QB, :] = total[n * QB : (n + 1) * QB, :]
        stats[n, 2 * QB : 3 * QB, :] = positive[n * QB : (n + 1) * QB, :]
    cand_store.wait()


def run_score(queries, meta_all, cand, item_counts):
    dma = pltpu.SemaphoreType.DMA
    return pl.pallas_call(
        score_kernel,
        out_shape=(
            jax.ShapeDtypeStruct((NJ, 3 * QB, 128), jnp.float32),
            jax.ShapeDtypeStruct((NC, SUB, E), jnp.bfloat16),
        ),
        in_specs=[ANY, ANY, ANY, VMEM],
        out_specs=(VMEM, ANY),
        scratch_shapes=[
            pltpu.VMEM((NJ * QROWS, E), jnp.bfloat16),
            pltpu.SMEM((NJ, 2 * QB, 128), jnp.int32),
            pltpu.VMEM((NJ, 2 * QB, 128), jnp.int32),
            pltpu.VMEM((NC, SUB, E), jnp.bfloat16),
            pltpu.VMEM((512, NC), jnp.float32),
            pltpu.VMEM((NC, SUB, 128), jnp.float32),
            pltpu.SMEM((NJ * QB * LIST + 2 * JOBS,), jnp.int32),
            pltpu.VMEM((NJ * QB + 8, 128), jnp.float32),
            pltpu.VMEM((NJ * QB + 8, 128), jnp.float32),
            pltpu.VMEM((NJ * QB + 8, 128), jnp.float32),
            dma((NJ,)),
            dma((4,)),
        ],
        compiler_params=pltpu.CompilerParams(vmem_limit_bytes=58 * 1024 * 1024),
        cost_estimate=pl.CostEstimate(flops=1 << 29, bytes_accessed=10 << 20, transcendentals=1 << 20),
        name="score",
    )(queries, meta_all, cand, item_counts)


def merged(parts):
    tops = [part[0] for part in parts]
    top = functools.reduce(jnp.maximum, tops)
    total = functools.reduce(jnp.add, [part[1] * jnp.exp(part[0] - top) for part in parts])
    positive = functools.reduce(jnp.add, [part[2] for part in parts])
    return top, total, positive


def thirds(ref, index):
    return tuple(ref[index, n * QB : (n + 1) * QB, :] for n in range(3))


def merge_kernel(stats, loss, by_group, part, by_catalog, send_a, recv_a, send_b, recv_b):
    t = lax.axis_index("catalog")
    x = lax.axis_index("query")
    d = lax.axis_index("dp")
    j = x * ND + d
    peers = [(dx, dd) for dx in range(NX) for dd in range(ND) if (dx, dd) != (0, 0)]

    def group_peer(n):
        dx, dd = peers[n]
        return (x + dx) % NX, (d + dd) % ND

    barrier = pltpu.get_barrier_semaphore()
    for n in range(NJ - 1):
        xp, dp = group_peer(n)
        pl.semaphore_signal(barrier, inc=1, device_id={"catalog": t, "query": xp, "dp": dp}, device_id_type=MESH)
    for k in range(1, NC):
        pl.semaphore_signal(barrier, inc=1, device_id={"catalog": flip(t, k, 4), "query": x, "dp": d}, device_id_type=MESH)
    pl.semaphore_wait(barrier, NJ - 1 + NC - 1)

    def group_copy(n):
        xp, dp = group_peer(n)
        return pltpu.make_async_remote_copy(
            src_ref=stats.at[xp * ND + dp],
            dst_ref=by_group.at[j],
            send_sem=send_a.at[n],
            recv_sem=recv_a.at[n],
            device_id={"catalog": t, "query": xp, "dp": dp},
            device_id_type=MESH,
        )

    for n in range(NJ - 1):
        group_copy(n).start()
    by_group[j] = stats[j]
    for n in range(NJ - 1):
        group_copy(n).wait_recv()
    for n, value in enumerate(merged([thirds(by_group, i) for i in range(NJ)])):
        part[n * QB : (n + 1) * QB, :] = value

    def catalog_copy(k):
        return pltpu.make_async_remote_copy(
            src_ref=part,
            dst_ref=by_catalog.at[t],
            send_sem=send_b.at[k],
            recv_sem=recv_b.at[k],
            device_id={"catalog": flip(t, k, 4), "query": x, "dp": d},
            device_id_type=MESH,
        )

    for k in range(NC - 1, 0, -1):
        catalog_copy(k).start()
    by_catalog[t] = part[...]
    for k in range(NC - 1, 0, -1):
        catalog_copy(k).wait_recv()
    top, total, positive = merged([thirds(by_catalog, i) for i in range(NC)])
    loss[...] = top + jnp.log(total) - positive
    for n in range(NJ - 1):
        group_copy(n).wait_send()
    for k in range(1, NC):
        catalog_copy(k).wait_send()


def run_merge(stats):
    dma = pltpu.SemaphoreType.DMA
    return pl.pallas_call(
        merge_kernel,
        out_shape=jax.ShapeDtypeStruct((QB, 128), jnp.float32),
        in_specs=[VMEM],
        out_specs=VMEM,
        scratch_shapes=[
            pltpu.VMEM((NJ, 3 * QB, 128), jnp.float32),
            pltpu.VMEM((3 * QB, 128), jnp.float32),
            pltpu.VMEM((NC, 3 * QB, 128), jnp.float32),
            dma((NJ - 1,)),
            dma((NJ - 1,)),
            dma((NC,)),
            dma((NC,)),
        ],
        compiler_params=pltpu.CompilerParams(collective_id=1, has_side_effects=True, vmem_limit_bytes=16 * 1024 * 1024),
        name="merge",
    )(stats)


def per_device(
    slab, fetch_rows, w_in, b_in, w_out, query_emb, item_counts, tile_blocks, tile_count, pos_idx
):
    queries, meta_all, cand = run_tower(
        fetch_rows, slab, query_emb, pos_idx.reshape(QB, 128), tile_blocks, tile_count, w_in, b_in.reshape(1, H), w_out
    )
    stats, cand = run_score(queries, meta_all, cand, item_counts.reshape(NC, 512))
    loss = run_merge(stats)
    return (cand[None], loss.reshape(QROWS))


def solution(mesh):
    in_specs = (
        P("catalog", None),
        P("catalog", None, ("query", "dp")),
        P(),
        P(),
        P(),
        P(("query", "dp"), None),
        P("catalog", None, None),
        P(("query", "dp"), "catalog", None),
        P(("query", "dp"), "catalog"),
        P(("query", "dp")),
    )
    out_specs = (P("catalog", None, ("query", "dp"), None), P(("query", "dp")))
    return jax.shard_map(
        per_device, mesh=mesh, in_specs=in_specs, out_specs=out_specs, check_vma=False
    )
```

```python
import functools

import jax
import jax.numpy as jnp
from jax import lax
from jax.experimental import pallas as pl
from jax.experimental.pallas import tpu as pltpu
from jax.sharding import PartitionSpec as P

MESH = pl.DeviceIdType.MESH
ANY = pl.BlockSpec(memory_space=pl.ANY)
VMEM = pl.BlockSpec(memory_space=pltpu.VMEM)
SMEM = pl.BlockSpec(memory_space=pltpu.SMEM)

E = 512
H = 2048
NC = 16
NX = 4
ND = 2
NJ = NX * ND
SUB = 64
LIST = 8
ROWS = 16384
QROWS = 1024
QB = QROWS // 128
HALF = QROWS // 2
SLAB_CHUNK = 512
OWNERS = 2
LOW = -1e30


def flip(value, bits, width):
    out = value
    for bit in range(width):
        if (bits >> bit) & 1:
            out = out + (1 << bit) * (1 - 2 * ((value // (1 << bit)) % 2))
    return out


FLOWS = (
    ("y", (0, 0), 0, 256, None),
    ("r", (0, 0), 0, 256, None),
    ("l", (0, 0), 256, 256, None),
    ("y", (0, 0), 256, 256, None),
    ("r", (0, 0), 256, 256, None),
    ("l", (0, 0), 0, 256, None),
    ("r", (-1, 0), 0, 256, 1),
    ("l", (1, 0), 256, 256, 2),
    ("r", (0, 1), 0, 256, 0),
    ("l", (0, 1), 0, 256, 0),
    ("y", (1, 0), 256, 256, 2),
    ("y", (-1, 0), 256, 256, 4),
    ("y", (2, 0), 256, 256, 7),
    ("r", (-1, 1), 0, 128, 8),
    ("l", (1, 1), 128, 128, 9),
)


def landed(flow):
    hop, (ox, oy), *_ = FLOWS[flow]
    ox, oy = {"r": (ox - 1, oy), "l": (ox + 1, oy), "y": (ox, 1 - oy)}[hop]
    return (2 if ox == -2 else ox), oy


def merged(parts):
    tops = [part[0] for part in parts]
    top = functools.reduce(jnp.maximum, tops)
    total = functools.reduce(jnp.add, [part[1] * jnp.exp(part[0] - top) for part in parts])
    positive = functools.reduce(jnp.add, [part[2] for part in parts])
    return top, total, positive


def thirds(ref, index):
    return tuple(ref[index, n * QB : (n + 1) * QB, :] for n in range(3))


def thirds(ref, index):
    return tuple(ref[index, n] for n in range(3))


def kernel(
    fetch, slab, query, pos, lists, counts, item_counts, w_in, b_in, w_out,
    cand_out, loss,
    chunk, table, rowbuf, staged, arrived, meta, meta_all, w_in_v, w_out_v, cand, queries, logt, neg_log, member, wanted,
    stats, by_group, part, by_catalog,
    slab_sem, w_sem, own_sem, meta_send, meta_recv, a2a_send, a2a_recv, flow_send, flow_recv, core_send, core_recv, out_sem,
    send_a, recv_a, send_b, recv_b,
):
    t = lax.axis_index("catalog")
    x = lax.axis_index("query")
    d = lax.axis_index("dp")
    core = t % 2
    j = x * ND + d

    own_query = pltpu.make_async_copy(query, queries.at[j], own_sem.at[0])
    n_chunks = ROWS // SLAB_CHUNK
    depth = chunk.shape[0]

    def slab_copy(n):
        slot = n % depth
        rows = pl.ds(pl.multiple_of(n * SLAB_CHUNK, SLAB_CHUNK), SLAB_CHUNK)
        return pltpu.make_async_copy(slab.at[rows], chunk.at[slot], slab_sem.at[slot])

    for n in range(depth):
        slab_copy(n).start()

    own_query.start()

    meta_peers = [(dx, dd) for dx in range(NX) for dd in range(ND) if (dx, dd) != (0, 0)]
    right, left = (x + 1) % NX, (x + NX - 1) % NX
    hop_to = {
        "r": {"catalog": t, "query": right, "dp": d},
        "l": {"catalog": t, "query": left, "dp": d},
        "y": {"catalog": flip(t, 8, 4), "query": x, "dp": 1 - d},
    }
    sibling = {"catalog": flip(t, 1, 4), "query": x, "dp": d}

    barrier = pltpu.get_barrier_semaphore()
    n_peers = 0
    for k in range(1, NC):
        pl.semaphore_signal(barrier, inc=1, device_id={"catalog": flip(t, k, 4), "query": x, "dp": d}, device_id_type=MESH)
        n_peers += 1
    for dx, dd in meta_peers:
        pl.semaphore_signal(
            barrier, inc=1, device_id={"catalog": t, "query": (x + dx) % NX, "dp": (d + dd) % ND}, device_id_type=MESH
        )
        n_peers += 1
    pl.semaphore_signal(barrier, inc=1, device_id=hop_to["y"], device_id_type=MESH)
    n_peers += 1

    square = (QB, LIST)
    diagonal = lax.broadcasted_iota(jnp.int32, square, 0) == lax.broadcasted_iota(jnp.int32, square, 1)
    count = jnp.sum(jnp.where(diagonal, jnp.broadcast_to(counts[...], square), 0), axis=1, keepdims=True)
    listed = jnp.where(lax.broadcasted_iota(jnp.int32, square, 1) < count, lists[:, 0, :], -1)
    meta[...] = jnp.full_like(meta, -1)
    meta[0:QB, :] = pos[...]
    meta[QB : 2 * QB, 0:LIST] = listed

    @pl.loop(0, n_chunks)
    def _(n):
        slot = n % depth
        slab_copy(n).wait()

        @pl.loop(0, SLAB_CHUNK // 64)
        def _(i):
            rows = pl.ds(pl.multiple_of(i * 64, 64), 64)
            to = pl.ds(pl.multiple_of(n * SLAB_CHUNK + i * 64, 64), 64)
            table[to, :] = chunk[slot, rows, :].astype(jnp.float32)

        @pl.when(n + depth < n_chunks)
        def _():
            slab_copy(n + depth).start()

    pl.semaphore_wait(barrier, n_peers)

    def origin(place):
        ox, oy = place
        xo = (x + ox + NX) % NX
        return xo * ND + (1 - d if oy else d)

    def flow_copy(n):
        hop, place, first, count, _ = FLOWS[n]
        jo = origin(place)
        rows = pl.ds(pl.multiple_of(core * HALF + first, 128), count)
        src = query.at[rows] if place == (0, 0) else queries.at[jo, rows]
        return pltpu.make_async_remote_copy(
            src_ref=src,
            dst_ref=queries.at[jo, rows],
            send_sem=flow_send.at[n],
            recv_sem=flow_recv.at[n],
            device_id=hop_to[hop],
            device_id_type=MESH,
        )

    def core_copy(n):
        _, _, first, count, _ = FLOWS[n]
        jo = origin(landed(n))
        rows = pl.ds(pl.multiple_of(core * HALF + first, 128), count)
        return pltpu.make_async_remote_copy(
            src_ref=queries.at[jo, rows],
            dst_ref=queries.at[jo, rows],
            send_sem=core_send.at[n],
            recv_sem=core_recv.at[n],
            device_id=sibling,
            device_id_type=MESH,
        )

    def advance(flows):
        for n in flows:
            flow_copy(n).wait_recv()
            for later, flow in enumerate(FLOWS):
                if flow[4] == n:
                    flow_copy(later).start()
            core_copy(n).start()

    for n, flow in enumerate(FLOWS):
        if flow[4] is None:
            flow_copy(n).start()

    def meta_copy(n):
        dx, dd = meta_peers[n]
        return pltpu.make_async_remote_copy(
            src_ref=meta,
            dst_ref=meta_all.at[j],
            send_sem=meta_send.at[n],
            recv_sem=meta_recv.at[n],
            device_id={"catalog": t, "query": (x + dx) % NX, "dp": (d + dd) % ND},
            device_id_type=MESH,
        )

    for n in range(len(meta_peers)):
        meta_copy(n).start()
    w_in_copy = pltpu.make_async_copy(w_in, w_in_v, w_sem.at[0])
    w_out_copy = pltpu.make_async_copy(w_out, w_out_v, w_sem.at[1])
    w_in_copy.start()
    w_out_copy.start()

    def a2a_copy(k):
        to = flip(t, k, 4)
        return pltpu.make_async_remote_copy(
            src_ref=staged.at[k],
            dst_ref=arrived.at[t],
            send_sem=a2a_send.at[k],
            recv_sem=a2a_recv.at[k],
            device_id={"catalog": to, "query": x, "dp": d},
            device_id_type=MESH,
        )

    for k in range(NC - 1, -1, -1):
        to = flip(t, k, 4)

        @pl.loop(0, SUB // 16)
        def _(i):
            for u in range(16):
                row = fetch[0, to, i * 16 + u]
                rowbuf[pl.ds(i * 16 + u, 1), :] = table[pl.ds(row, 1), :]

        if k:
            staged[k] = rowbuf[...].astype(jnp.bfloat16)
            a2a_copy(k).start()
        else:
            arrived[t] = rowbuf[...].astype(jnp.bfloat16)

    advance((0, 1, 2))
    w_in_copy.wait()
    w_out_copy.wait()

    def tower(group):
        base = 4 * flip(t // 4, group, 2)
        for k in range(4 * group, 4 * group + 4):
            if k:
                a2a_copy(k).wait_recv()
        rows = arrived[pl.ds(base, 4)].reshape(4 * SUB, E)
        hidden = jnp.maximum(jnp.dot(rows, w_in_v[...], preferred_element_type=jnp.float32) + b_in[...], 0.0).astype(jnp.bfloat16)
        y = jnp.dot(hidden, w_out_v[...], preferred_element_type=jnp.float32)
        normed = y * lax.rsqrt(jnp.sum(y * y, axis=-1, keepdims=True) + 1e-06)
        cand[pl.ds(base, 4)] = normed.astype(jnp.bfloat16).reshape(4, SUB, E)
        pltpu.make_async_copy(cand.at[pl.ds(base, 4)], cand_out.at[pl.ds(base, 4)], out_sem.at[group]).start()

    logt[...] = jnp.transpose(-jnp.log(item_counts[...].astype(jnp.float32)))
    own = logt[pl.ds(pl.multiple_of(j * SUB, SUB), SUB), :]
    for o in range(NC):
        neg_log[o * SUB : (o + 1) * SUB, :] = jnp.broadcast_to(own[:, o : o + 1], (SUB, 128))

    for n in range(len(meta_peers)):
        meta_copy(n).wait_recv()
    meta_all[j] = meta[...]
    owner_block = lax.broadcasted_iota(jnp.int32, (NC, 128), 0) * 4 + x

    @pl.loop(0, NJ)
    def _(jo):
        offset = meta_all[jo, 0:QB, :] - (t * (NC * 512) + j * SUB)
        here = (offset >= 0) & (offset < NC * 512) & ((offset & 511) < SUB)
        wanted[jo] = jnp.where(here, (offset >> 9) * SUB + (offset & 511), -1)
        for b in range(QB):
            row = meta_all[jo, QB + b : QB + b + 1, :]
            hit = jnp.zeros((NC, 128), jnp.int32)
            for e in range(LIST):
                hit = hit | (jnp.broadcast_to(row[:, e : e + 1], (NC, 128)) == owner_block).astype(jnp.int32)
            member[jo, b] = hit

    tower(0)
    advance((3, 4, 5))
    tower(1)
    advance((7, 6, 8, 9))
    tower(2)
    tower(3)

    row_ids = lax.broadcasted_iota(jnp.int32, (8, 128), 0)
    wide = OWNERS * SUB

    def score(place):
        jo = origin(place)

        @pl.loop(0, QB // 2)
        def _(pair):
            rows = queries[jo, pl.ds(pl.multiple_of(pair * 256, 256), 256), :]
            low = jnp.full((8, 128), LOW, jnp.float32)
            top, total, positive = [low, low], [jnp.zeros_like(low)] * 2, [jnp.zeros_like(low)] * 2
            want = [jnp.broadcast_to(wanted[jo, pl.ds(pair * 2 + h, 1), :], (8, 128)) for h in range(2)]
            for step in range(NC // OWNERS):
                scores = lax.dot_general(
                    cand[step * OWNERS : (step + 1) * OWNERS].reshape(wide, E),
                    rows,
                    (((1,), (1,)), ((), ())),
                    preferred_element_type=jnp.float32,
                )
                for h in range(2):
                    tiles, peak = [], low
                    for o in range(OWNERS):
                        owner = step * OWNERS + o
                        mine = []
                        for i in range(SUB // 8):
                            at = o * SUB + i * 8
                            tile = scores[at : at + 8, h * 128 : (h + 1) * 128]
                            tile = tile + neg_log[step * wide + at : step * wide + at + 8, :]
                            positive[h] = jnp.where(row_ids == want[h] - (step * wide + at), tile, positive[h])
                            mine.append(tile)
                        hit = jnp.broadcast_to(member[jo, pair * 2 + h, owner : owner + 1, :], (8, 128)) > 0
                        peak = jnp.maximum(peak, jnp.where(hit, functools.reduce(jnp.maximum, mine), LOW))
                        tiles.append((hit, mine))
                    mass = jnp.zeros_like(low)
                    for hit, mine in tiles:
                        mass = mass + jnp.where(hit, functools.reduce(jnp.add, [jnp.exp(tile - peak) for tile in mine]), 0.0)
                    new = jnp.maximum(top[h], peak)
                    total[h] = total[h] * jnp.exp(top[h] - new) + mass * jnp.exp(peak - new)
                    top[h] = new
            for h in range(2):
                peak = jnp.max(top[h], axis=0, keepdims=True)
                at = pl.ds(pair * 2 + h, 1)
                stats[jo, 0, at, :] = peak
                stats[jo, 1, at, :] = jnp.sum(total[h] * jnp.exp(top[h] - peak), axis=0, keepdims=True)
                stats[jo, 2, at, :] = jnp.sum(positive[h], axis=0, keepdims=True)

    def group_copy(place):
        ox, oy = place
        n = meta_peers.index(((ox + NX) % NX, oy))
        jo = origin(place)
        return pltpu.make_async_remote_copy(
            src_ref=stats.at[jo],
            dst_ref=by_group.at[j],
            send_sem=send_a.at[n],
            recv_sem=recv_a.at[n],
            device_id={"catalog": t, "query": (x + ox + NX) % NX, "dp": 1 - d if oy else d},
            device_id_type=MESH,
        )

    def finish(place):
        for n in range(len(FLOWS)):
            if landed(n) == place:
                core_copy(n).wait_recv()
        score(place)
        group_copy(place).start()

    own_query.wait()
    score((0, 0))
    finish((0, 1))
    finish((1, 0))
    advance((10, 11, 12))
    finish((-1, 0))
    advance((13, 14))
    finish((2, 0))
    finish((1, 1))
    finish((-1, 1))
    finish((2, 1))

    by_group[j] = stats[j]
    places = [(0, 1), (1, 0), (-1, 0), (2, 0), (1, 1), (-1, 1), (2, 1)]
    for place in places:
        group_copy(place).wait_recv()
    for n, value in enumerate(merged([thirds(by_group, i) for i in range(NJ)])):
        part[n] = value

    def catalog_copy(k):
        return pltpu.make_async_remote_copy(
            src_ref=part,
            dst_ref=by_catalog.at[t],
            send_sem=send_b.at[k],
            recv_sem=recv_b.at[k],
            device_id={"catalog": flip(t, k, 4), "query": x, "dp": d},
            device_id_type=MESH,
        )

    for k in range(NC - 1, 0, -1):
        catalog_copy(k).start()
    by_catalog[t] = part[...]

    for group in range(4):
        base = 4 * flip(t // 4, group, 2)
        pltpu.make_async_copy(cand.at[pl.ds(base, 4)], cand_out.at[pl.ds(base, 4)], out_sem.at[group]).wait()
    for k in range(1, NC):
        a2a_copy(k).wait_send()
    for n in range(len(FLOWS)):
        flow_copy(n).wait_send()
        core_copy(n).wait_send()
    for n in range(len(meta_peers)):
        meta_copy(n).wait_send()
    for place in places:
        group_copy(place).wait_send()

    for k in range(NC - 1, 0, -1):
        catalog_copy(k).wait_recv()
    top, total, positive = merged([thirds(by_catalog, i) for i in range(NC)])
    loss[...] = top + jnp.log(total) - positive
    for k in range(1, NC):
        catalog_copy(k).wait_send()


def per_device(
    slab, fetch_rows, w_in, b_in, w_out, query_emb, item_counts, tile_blocks, tile_count, pos_idx
):
    dma = pltpu.SemaphoreType.DMA
    bf16, f32, i32 = jnp.bfloat16, jnp.float32, jnp.int32
    cand, loss = pl.pallas_call(
        kernel,
        out_shape=(
            jax.ShapeDtypeStruct((NC, SUB, E), bf16),
            jax.ShapeDtypeStruct((QB, 128), f32),
        ),
        in_specs=[SMEM, ANY, ANY, VMEM, VMEM, VMEM, VMEM, ANY, VMEM, ANY],
        out_specs=(ANY, VMEM),
        scratch_shapes=[
            pltpu.VMEM((4, SLAB_CHUNK, E), bf16),
            pltpu.VMEM((ROWS, E), f32),
            pltpu.VMEM((SUB, E), f32),
            pltpu.VMEM((NC, SUB, E), bf16),
            pltpu.VMEM((NC, SUB, E), bf16),
            pltpu.VMEM((2 * QB, 128), i32),
            pltpu.VMEM((NJ, 2 * QB, 128), i32),
            pltpu.VMEM((E, H), bf16),
            pltpu.VMEM((H, E), bf16),
            pltpu.VMEM((NC, SUB, E), bf16),
            pltpu.VMEM((NJ, QROWS, E), bf16),
            pltpu.VMEM((512, NC), f32),
            pltpu.VMEM((NC * SUB, 128), f32),
            pltpu.VMEM((NJ, QB, NC, 128), i32),
            pltpu.VMEM((NJ, QB, 128), i32),
            pltpu.VMEM((NJ, 3, QB, 128), f32),
            pltpu.VMEM((NJ, 3, QB, 128), f32),
            pltpu.VMEM((3, QB, 128), f32),
            pltpu.VMEM((NC, 3, QB, 128), f32),
            dma((4,)),
            dma((2,)),
            dma((1,)),
            dma((NJ - 1,)),
            dma((NJ - 1,)),
            dma((NC,)),
            dma((NC,)),
            dma((len(FLOWS),)),
            dma((len(FLOWS),)),
            dma((len(FLOWS),)),
            dma((len(FLOWS),)),
            dma((4,)),
            dma((NJ - 1,)),
            dma((NJ - 1,)),
            dma((NC,)),
            dma((NC,)),
        ],
        compiler_params=pltpu.CompilerParams(
            collective_id=0, has_side_effects=True, vmem_limit_bytes=60 * 1024 * 1024
        ),
        cost_estimate=pl.CostEstimate(flops=12 << 30, bytes_accessed=32 << 20, transcendentals=1 << 23),
        name="two_tower",
    )(
        fetch_rows,
        slab,
        query_emb,
        pos_idx.reshape(QB, 128),
        tile_blocks,
        tile_count.reshape(1, QB),
        item_counts.reshape(NC, 512),
        w_in,
        b_in.reshape(1, H),
        w_out,
    )
    return (cand[None], loss.reshape(QROWS))


def solution(mesh):
    in_specs = (
        P("catalog", None),
        P("catalog", None, ("query", "dp")),
        P(),
        P(),
        P(),
        P(("query", "dp"), None),
        P("catalog", None, None),
        P(("query", "dp"), "catalog", None),
        P(("query", "dp"), "catalog"),
        P(("query", "dp")),
    )
    out_specs = (P("catalog", None, ("query", "dp"), None), P(("query", "dp")))
    return jax.shard_map(
        per_device, mesh=mesh, in_specs=in_specs, out_specs=out_specs, check_vma=False
    )
```

```python
import functools

import jax
import jax.numpy as jnp
from jax import lax
from jax.experimental import pallas as pl
from jax.experimental.pallas import tpu as pltpu
from jax.sharding import PartitionSpec as P

MESH = pl.DeviceIdType.MESH
ANY = pl.BlockSpec(memory_space=pl.ANY)
VMEM = pl.BlockSpec(memory_space=pltpu.VMEM)
SMEM = pl.BlockSpec(memory_space=pltpu.SMEM)

E = 512
H = 2048
NC = 16
NX = 4
ND = 2
NJ = NX * ND
SUB = 64
LIST = 8
ROWS = 16384
QROWS = 1024
QB = QROWS // 128
HALF = QROWS // 2
SLAB_CHUNK = 1024
JOBS = 4
NONE = 256
LOW = -1e30
VMEM_LIMIT = 60 * 1024 * 1024


def flip(value, bits, width):
    out = value
    for bit in range(width):
        if (bits >> bit) & 1:
            out = out + (1 << bit) * (1 - 2 * ((value // (1 << bit)) % 2))
    return out


FLOWS = {}
for _n in (0, 128):
    FLOWS |= {
        f"y{_n}": ("y", (0, 0), _n, 128, None),
        f"r{_n}": ("r", (0, 0), _n, 128, None),
        f"l{_n + 256}": ("l", (0, 0), _n + 256, 128, None),
    }
for _n in (0, 128):
    FLOWS |= {
        f"y{_n + 256}": ("y", (0, 0), _n + 256, 128, None),
        f"r{_n + 256}": ("r", (0, 0), _n + 256, 128, None),
        f"l{_n}": ("l", (0, 0), _n, 128, None),
    }
for _n in (0, 128):
    FLOWS |= {
        f"rr{_n}": ("r", (-1, 0), _n, 128, f"r{_n}"),
        f"ll{_n + 256}": ("l", (1, 0), _n + 256, 128, f"l{_n + 256}"),
        f"yr{_n}": ("r", (0, 1), _n, 128, f"y{_n}"),
        f"yl{_n}": ("l", (0, 1), _n, 128, f"y{_n}"),
        f"ly{_n}": ("y", (1, 0), _n + 256, 128, f"l{_n + 256}"),
        f"ry{_n}": ("y", (-1, 0), _n + 256, 128, f"r{_n + 256}"),
        f"lly{_n}": ("y", (2, 0), _n + 256, 128, f"ll{_n + 256}"),
    }
FLOWS |= {
    "yrr": ("r", (-1, 1), 0, 128, "yr0"),
    "yll": ("l", (1, 1), 128, 128, "yl128"),
}
NAMES = tuple(FLOWS)
PLACES = ((0, 0), (0, 1), (1, 0), (-1, 0), (2, 0), (1, 1), (-1, 1), (2, 1))


def landed(name):
    hop, (ox, oy), *_ = FLOWS[name]
    ox, oy = {"r": (ox - 1, oy), "l": (ox + 1, oy), "y": (ox, 1 - oy)}.get(hop, (ox, oy))
    return (2 if ox == -2 else ox), oy


def tower_kernel(
    fetch, slab, query, pos, lists, counts, item_counts, w_in, b_in, w_out,
    queries_out, meta_all, wanted, neg_log, cand,
    queries, chunk, table, rowbuf, staged, arrived, meta, w_in_v, w_out_v, logt,
    slab_sem, w_sem, own_sem, meta_send, meta_recv, a2a_send, a2a_recv, flow_send, flow_recv, core_send, core_recv, out_sem,
):
    t = lax.axis_index("catalog")
    x = lax.axis_index("query")
    d = lax.axis_index("dp")
    core = t % 2
    j = x * ND + d

    own_query = pltpu.make_async_copy(query, queries.at[j], own_sem.at[0])
    n_chunks = ROWS // SLAB_CHUNK
    depth = chunk.shape[0]

    def slab_copy(n):
        slot = n % depth
        rows = pl.ds(pl.multiple_of(n * SLAB_CHUNK, SLAB_CHUNK), SLAB_CHUNK)
        return pltpu.make_async_copy(slab.at[rows], chunk.at[slot], slab_sem.at[slot])

    for n in range(depth):
        slab_copy(n).start()

    own_query.start()

    meta_peers = [(dx, dd) for dx in range(NX) for dd in range(ND) if (dx, dd) != (0, 0)]
    right, left = (x + 1) % NX, (x + NX - 1) % NX
    hop_to = {
        "r": {"catalog": t, "query": right, "dp": d},
        "l": {"catalog": t, "query": left, "dp": d},
        "y": {"catalog": flip(t, 8, 4), "query": x, "dp": 1 - d},
    }
    sibling = {"catalog": flip(t, 1, 4), "query": x, "dp": d}

    barrier = pltpu.get_barrier_semaphore()
    n_peers = 0
    for k in range(1, NC):
        pl.semaphore_signal(barrier, inc=1, device_id={"catalog": flip(t, k, 4), "query": x, "dp": d}, device_id_type=MESH)
        n_peers += 1
    for dx, dd in meta_peers:
        pl.semaphore_signal(
            barrier, inc=1, device_id={"catalog": t, "query": (x + dx) % NX, "dp": (d + dd) % ND}, device_id_type=MESH
        )
        n_peers += 1
    pl.semaphore_signal(barrier, inc=1, device_id=hop_to["y"], device_id_type=MESH)
    n_peers += 1

    square = (QB, LIST)
    diagonal = lax.broadcasted_iota(jnp.int32, square, 0) == lax.broadcasted_iota(jnp.int32, square, 1)
    count = jnp.sum(jnp.where(diagonal, jnp.broadcast_to(counts[...], square), 0), axis=1, keepdims=True)
    listed = jnp.where(lax.broadcasted_iota(jnp.int32, square, 1) < count, lists[:, 0, :], NONE)
    meta[...] = jnp.full_like(meta, NONE)
    meta[0:QB, :] = pos[...]
    meta[QB : 2 * QB, 0:LIST] = listed

    pl.semaphore_wait(barrier, n_peers)

    def origin(place):
        ox, oy = place
        xo = (x + ox + NX) % NX
        return xo * ND + (1 - d if oy else d)

    def flow_copy(name):
        hop, place, first, count, _ = FLOWS[name]
        jo = origin(place)
        rows = pl.ds(pl.multiple_of(core * HALF + first, 128), count)
        src = query.at[rows] if place == (0, 0) else queries.at[jo, rows]
        return pltpu.make_async_remote_copy(
            src_ref=src,
            dst_ref=queries.at[jo, rows],
            send_sem=flow_send.at[NAMES.index(name)],
            recv_sem=flow_recv.at[NAMES.index(name)],
            device_id=hop_to[hop],
            device_id_type=MESH,
        )

    def core_copy(name):
        _, _, first, count, _ = FLOWS[name]
        part = queries.at[origin(landed(name)), pl.ds(pl.multiple_of(core * HALF + first, 128), count)]
        return pltpu.make_async_remote_copy(
            src_ref=part,
            dst_ref=part,
            send_sem=core_send.at[NAMES.index(name)],
            recv_sem=core_recv.at[NAMES.index(name)],
            device_id=sibling,
            device_id_type=MESH,
        )

    received, sent = set(), set()

    def send_ready():
        for name, flow in FLOWS.items():
            if name not in sent and (flow[4] is None or flow[4] in received):
                sent.add(name)
                flow_copy(name).start()

    def advance(*names):
        for name in names:
            flow_copy(name).wait_recv()
            received.add(name)
            send_ready()
            core_copy(name).start()

    send_ready()

    def meta_copy(n):
        dx, dd = meta_peers[n]
        return pltpu.make_async_remote_copy(
            src_ref=meta,
            dst_ref=meta_all.at[j],
            send_sem=meta_send.at[n],
            recv_sem=meta_recv.at[n],
            device_id={"catalog": t, "query": (x + dx) % NX, "dp": (d + dd) % ND},
            device_id_type=MESH,
        )

    for n in range(len(meta_peers)):
        meta_copy(n).start()
    def widen(first, count):
        @pl.loop(first, first + count)
        def _(n):
            slot = n % depth
            slab_copy(n).wait()

            @pl.loop(0, SLAB_CHUNK // 64)
            def _(i):
                rows = pl.ds(pl.multiple_of(i * 64, 64), 64)
                to = pl.ds(pl.multiple_of(n * SLAB_CHUNK + i * 64, 64), 64)
                table[to, :] = chunk[slot, rows, :].astype(jnp.float32)

            @pl.when(n + depth < n_chunks)
            def _():
                slab_copy(n + depth).start()

    widen(0, n_chunks // 2)
    advance("y0", "r0", "l256")
    widen(n_chunks // 2, n_chunks // 2)
    w_in_copy = pltpu.make_async_copy(w_in, w_in_v, w_sem.at[0])
    w_out_copy = pltpu.make_async_copy(w_out, w_out_v, w_sem.at[1])
    w_in_copy.start()
    w_out_copy.start()

    def a2a_copy(k):
        to = flip(t, k, 4)
        return pltpu.make_async_remote_copy(
            src_ref=staged.at[k],
            dst_ref=arrived.at[t],
            send_sem=a2a_send.at[k],
            recv_sem=a2a_recv.at[k],
            device_id={"catalog": to, "query": x, "dp": d},
            device_id_type=MESH,
        )

    for k in range(NC - 1, -1, -1):
        to = flip(t, k, 4)

        @pl.loop(0, SUB // 16)
        def _(i):
            for u in range(16):
                row = fetch[0, to, i * 16 + u]
                rowbuf[pl.ds(i * 16 + u, 1), :] = table[pl.ds(row, 1), :]

        if k:
            staged[k] = rowbuf[...].astype(jnp.bfloat16)
        else:
            arrived[t] = rowbuf[...].astype(jnp.bfloat16)
        if k == 12:
            advance("y128", "r128", "l384")
        if k == 6:
            advance("r256", "l0", "y256")
        if k:
            a2a_copy(k).start()

    advance("rr0", "ll256", "yr0", "yl0", "r384", "l128", "y384")
    w_in_copy.wait()
    w_out_copy.wait()

    def tower(group):
        base = 4 * flip(t // 4, group, 2)
        for k in range(4 * group, 4 * group + 4):
            if k:
                a2a_copy(k).wait_recv()
        rows = arrived[pl.ds(base, 4)].reshape(4 * SUB, E)
        hidden = jnp.maximum(jnp.dot(rows, w_in_v[...], preferred_element_type=jnp.float32) + b_in[...], 0.0).astype(jnp.bfloat16)
        y = jnp.dot(hidden, w_out_v[...], preferred_element_type=jnp.float32)
        normed = y * lax.rsqrt(jnp.sum(y * y, axis=-1, keepdims=True) + 1e-06)
        cand[pl.ds(base, 4)] = normed.astype(jnp.bfloat16).reshape(4, SUB, E)

    logt[...] = jnp.transpose(-jnp.log(item_counts[...].astype(jnp.float32)))
    own = logt[pl.ds(pl.multiple_of(j * SUB, SUB), SUB), :]
    for o in range(NC):
        neg_log[o * SUB : (o + 1) * SUB, :] = jnp.broadcast_to(own[:, o : o + 1], (SUB, 128))

    for n in range(len(meta_peers)):
        meta_copy(n).wait_recv()
    meta_all[j] = meta[...]
    for jo in range(NJ):
        offset = meta_all[jo, 0:QB, :] - (t * (NC * 512) + j * SUB)
        here = (offset >= 0) & (offset < NC * 512) & ((offset & 511) < SUB)
        wanted[jo] = jnp.where(here, (offset >> 9) * SUB + (offset & 511), -1)

    def query_out(place):
        jo = origin(place)
        return pltpu.make_async_copy(queries.at[jo], queries_out.at[jo], out_sem.at[PLACES.index(place)])

    def ship(*places):
        for place in places:
            for name in NAMES:
                if landed(name) == place:
                    core_copy(name).wait_recv()
            query_out(place).start()

    own_query.wait()
    query_out((0, 0)).start()
    advance("ly0", "ry0", "rr128", "ll384")
    tower(0)
    ship((0, 1), (1, 0), (-1, 0))
    advance("yr128", "yl128")
    tower(1)
    ship((2, 0))
    advance("ly128", "ry128", "lly0")
    tower(2)
    ship((1, 1), (-1, 1))
    tower(3)
    advance("yrr", "yll", "lly128")
    ship((2, 1))
    assert len(received) == len(sent) == len(NAMES)

    for place in PLACES:
        query_out(place).wait()
    for k in range(1, NC):
        a2a_copy(k).wait_send()
    for name in NAMES:
        flow_copy(name).wait_send()
        core_copy(name).wait_send()
    for n in range(len(meta_peers)):
        meta_copy(n).wait_send()


def run_tower(fetch, slab, query, pos, lists, counts, item_counts, w_in, b_in, w_out):
    dma = pltpu.SemaphoreType.DMA
    bf16, f32, i32 = jnp.bfloat16, jnp.float32, jnp.int32
    return pl.pallas_call(
        tower_kernel,
        out_shape=(
            jax.ShapeDtypeStruct((NJ, QROWS, E), bf16),
            jax.ShapeDtypeStruct((NJ, 2 * QB, 128), i32),
            jax.ShapeDtypeStruct((NJ, QB, 128), i32),
            jax.ShapeDtypeStruct((NC * SUB, 128), f32),
            jax.ShapeDtypeStruct((NC, SUB, E), bf16),
        ),
        in_specs=[SMEM, ANY, ANY, VMEM, VMEM, VMEM, VMEM, ANY, VMEM, ANY],
        out_specs=(ANY, VMEM, VMEM, VMEM, VMEM),
        scratch_shapes=[
            pltpu.VMEM((NJ, QROWS, E), bf16),
            pltpu.VMEM((8, SLAB_CHUNK, E), bf16),
            pltpu.VMEM((ROWS, E), f32),
            pltpu.VMEM((SUB, E), f32),
            pltpu.VMEM((NC, SUB, E), bf16),
            pltpu.VMEM((NC, SUB, E), bf16),
            pltpu.VMEM((2 * QB, 128), i32),
            pltpu.VMEM((E, H), bf16),
            pltpu.VMEM((H, E), bf16),
            pltpu.VMEM((512, NC), f32),
            dma((8,)),
            dma((2,)),
            dma((1,)),
            dma((NJ - 1,)),
            dma((NJ - 1,)),
            dma((NC,)),
            dma((NC,)),
            dma((len(NAMES),)),
            dma((len(NAMES),)),
            dma((len(NAMES),)),
            dma((len(NAMES),)),
            dma((NJ,)),
        ],
        compiler_params=pltpu.CompilerParams(
            collective_id=0, has_side_effects=True, vmem_limit_bytes=VMEM_LIMIT
        ),
        cost_estimate=pl.CostEstimate(flops=4 * 1024 * E * H, bytes_accessed=32 << 20, transcendentals=0),
        name="tower",
    )(fetch, slab, query, pos, lists, counts, item_counts, w_in, b_in, w_out)


def score_kernel(
    queries, meta, wanted, neg_log, cand,
    stats, cand_out,
    q, jobs, top, total, positive, q_sem, sem,
):
    x = lax.axis_index("query")
    cand_store = pltpu.make_async_copy(cand, cand_out, sem.at[0])
    loads = [pltpu.make_async_copy(queries.at[n], q.at[n], q_sem.at[n]) for n in range(NJ)]
    for load in loads:
        load.start()
    cand_store.start()

    top[...] = jnp.full_like(top, LOW)
    total[...] = jnp.zeros_like(total)
    positive[...] = jnp.zeros_like(positive)

    def list_blocks(jo, n):
        for b in range(QB):
            for e in range(LIST):
                block = meta[jo, QB + b, e]
                jobs[n] = (jo * QB + b) * NC + (block >> 2)
                n = n + jnp.where((block & (NONE + 3)) == x, 1, 0)
        return n

    n_jobs = lax.fori_loop(0, NJ, list_blocks, jnp.int32(0))
    for u in range(JOBS):
        jobs[n_jobs + u] = NJ * QB * NC

    for load in loads:
        load.wait()
    row_ids = lax.broadcasted_iota(jnp.int32, (SUB, 128), 0)

    @pl.loop(0, (n_jobs + JOBS - 1) // JOBS)
    def _(step):
        found = []
        for u in range(JOBS):
            job = jobs[step * JOBS + u]
            b, o = job >> 4, job & (NC - 1)
            b_q = jnp.minimum(b, NJ * QB - 1)
            jo, b_j = b_q >> 3, b_q & (QB - 1)
            block = q[jo, pl.ds(pl.multiple_of(b_j * 128, 128), 128), :]
            scores = lax.dot_general(cand[o], block, (((1,), (1,)), ((), ())), preferred_element_type=jnp.float32)
            scores = scores + neg_log[pl.ds(pl.multiple_of(o * SUB, SUB), SUB), :]
            want = wanted[jo, pl.ds(b_j, 1), :] - o * SUB
            peak = jnp.max(scores, axis=0, keepdims=True)
            mass = jnp.sum(jnp.exp(scores - peak), axis=0, keepdims=True)
            match = jnp.sum(jnp.where(row_ids == want, scores, 0.0), axis=0, keepdims=True)
            found.append((b, peak, mass, match))
        for b, peak, mass, match in found:
            at = pl.ds(b, 1)
            old = top[at, :]
            new = jnp.maximum(old, peak)
            total[at, :] = total[at, :] * jnp.exp(old - new) + mass * jnp.exp(peak - new)
            positive[at, :] = positive[at, :] + match
            top[at, :] = new

    for n in range(NJ):
        stats[n, 0:QB, :] = top[n * QB : (n + 1) * QB, :]
        stats[n, QB : 2 * QB, :] = total[n * QB : (n + 1) * QB, :]
        stats[n, 2 * QB : 3 * QB, :] = positive[n * QB : (n + 1) * QB, :]
    cand_store.wait()


def run_score(queries, meta, wanted, neg_log, cand):
    return pl.pallas_call(
        score_kernel,
        out_shape=(
            jax.ShapeDtypeStruct((NJ, 3 * QB, 128), jnp.float32),
            jax.ShapeDtypeStruct((NC, SUB, E), jnp.bfloat16),
        ),
        in_specs=[ANY, SMEM, VMEM, VMEM, VMEM],
        out_specs=(VMEM, ANY),
        scratch_shapes=[
            pltpu.VMEM((NJ, QROWS, E), jnp.bfloat16),
            pltpu.SMEM((NJ * QB * LIST + 2 * JOBS,), jnp.int32),
            pltpu.VMEM((NJ * QB + 8, 128), jnp.float32),
            pltpu.VMEM((NJ * QB + 8, 128), jnp.float32),
            pltpu.VMEM((NJ * QB + 8, 128), jnp.float32),
            pltpu.SemaphoreType.DMA((NJ,)),
            pltpu.SemaphoreType.DMA((1,)),
        ],
        compiler_params=pltpu.CompilerParams(vmem_limit_bytes=VMEM_LIMIT),
        cost_estimate=pl.CostEstimate(flops=1 << 29, bytes_accessed=10 << 20, transcendentals=1 << 20),
        name="score",
    )(queries, meta, wanted, neg_log, cand)


def merged(parts):
    tops = [part[0] for part in parts]
    top = functools.reduce(jnp.maximum, tops)
    total = functools.reduce(jnp.add, [part[1] * jnp.exp(part[0] - top) for part in parts])
    positive = functools.reduce(jnp.add, [part[2] for part in parts])
    return top, total, positive


def thirds(ref, index):
    return tuple(ref[index, n * QB : (n + 1) * QB, :] for n in range(3))


def merge_kernel(stats, loss, by_group, part, by_catalog, send_a, recv_a, send_b, recv_b):
    t = lax.axis_index("catalog")
    x = lax.axis_index("query")
    d = lax.axis_index("dp")
    j = x * ND + d
    peers = [(dx, dd) for dx in range(NX) for dd in range(ND) if (dx, dd) != (0, 0)]

    def group_peer(n):
        dx, dd = peers[n]
        return (x + dx) % NX, (d + dd) % ND

    barrier = pltpu.get_barrier_semaphore()
    for n in range(NJ - 1):
        xp, dp = group_peer(n)
        pl.semaphore_signal(barrier, inc=1, device_id={"catalog": t, "query": xp, "dp": dp}, device_id_type=MESH)
    for k in range(1, NC):
        pl.semaphore_signal(barrier, inc=1, device_id={"catalog": flip(t, k, 4), "query": x, "dp": d}, device_id_type=MESH)
    pl.semaphore_wait(barrier, NJ - 1 + NC - 1)

    def group_copy(n):
        xp, dp = group_peer(n)
        return pltpu.make_async_remote_copy(
            src_ref=stats.at[xp * ND + dp],
            dst_ref=by_group.at[j],
            send_sem=send_a.at[n],
            recv_sem=recv_a.at[n],
            device_id={"catalog": t, "query": xp, "dp": dp},
            device_id_type=MESH,
        )

    for n in range(NJ - 1):
        group_copy(n).start()
    by_group[j] = stats[j]
    for n in range(NJ - 1):
        group_copy(n).wait_recv()
    for n, value in enumerate(merged([thirds(by_group, i) for i in range(NJ)])):
        part[n * QB : (n + 1) * QB, :] = value

    def catalog_copy(k):
        return pltpu.make_async_remote_copy(
            src_ref=part,
            dst_ref=by_catalog.at[t],
            send_sem=send_b.at[k],
            recv_sem=recv_b.at[k],
            device_id={"catalog": flip(t, k, 4), "query": x, "dp": d},
            device_id_type=MESH,
        )

    for k in range(NC - 1, 0, -1):
        catalog_copy(k).start()
    by_catalog[t] = part[...]
    for k in range(NC - 1, 0, -1):
        catalog_copy(k).wait_recv()
    top, total, positive = merged([thirds(by_catalog, i) for i in range(NC)])
    loss[...] = top + jnp.log(total) - positive
    for n in range(NJ - 1):
        group_copy(n).wait_send()
    for k in range(1, NC):
        catalog_copy(k).wait_send()


def run_merge(stats):
    dma = pltpu.SemaphoreType.DMA
    return pl.pallas_call(
        merge_kernel,
        out_shape=jax.ShapeDtypeStruct((QB, 128), jnp.float32),
        in_specs=[VMEM],
        out_specs=VMEM,
        scratch_shapes=[
            pltpu.VMEM((NJ, 3 * QB, 128), jnp.float32),
            pltpu.VMEM((3 * QB, 128), jnp.float32),
            pltpu.VMEM((NC, 3 * QB, 128), jnp.float32),
            dma((NJ - 1,)),
            dma((NJ - 1,)),
            dma((NC,)),
            dma((NC,)),
        ],
        compiler_params=pltpu.CompilerParams(collective_id=1, has_side_effects=True, vmem_limit_bytes=16 * 1024 * 1024),
        name="merge",
    )(stats)


def per_device(
    slab, fetch_rows, w_in, b_in, w_out, query_emb, item_counts, tile_blocks, tile_count, pos_idx
):
    queries, meta, wanted, neg_log, cand = run_tower(
        fetch_rows,
        slab,
        query_emb,
        pos_idx.reshape(QB, 128),
        tile_blocks,
        tile_count.reshape(1, QB),
        item_counts.reshape(NC, 512),
        w_in,
        b_in.reshape(1, H),
        w_out,
    )
    stats, cand = run_score(queries, meta, wanted, neg_log, cand)
    loss = run_merge(stats)
    return (cand[None], loss.reshape(QROWS))


def solution(mesh):
    in_specs = (
        P("catalog", None),
        P("catalog", None, ("query", "dp")),
        P(),
        P(),
        P(),
        P(("query", "dp"), None),
        P("catalog", None, None),
        P(("query", "dp"), "catalog", None),
        P(("query", "dp"), "catalog"),
        P(("query", "dp")),
    )
    out_specs = (P("catalog", None, ("query", "dp"), None), P(("query", "dp")))
    return jax.shard_map(
        per_device, mesh=mesh, in_specs=in_specs, out_specs=out_specs, check_vma=False
    )
```

```python
import functools

import jax
import jax.numpy as jnp
from jax import lax
from jax.experimental import pallas as pl
from jax.experimental.pallas import tpu as pltpu
from jax.sharding import PartitionSpec as P

MESH = pl.DeviceIdType.MESH
ANY = pl.BlockSpec(memory_space=pl.ANY)
VMEM = pl.BlockSpec(memory_space=pltpu.VMEM)
SMEM = pl.BlockSpec(memory_space=pltpu.SMEM)

E = 512
H = 2048
NC = 16
NX = 4
ND = 2
NJ = NX * ND
SUB = 64
LIST = 8
ROWS = 16384
QROWS = 1024
QB = QROWS // 128
HALF = QROWS // 2
SLAB_CHUNK = 1024
JOBS = 8
NONE = 256
LOW = -1e30
VMEM_LIMIT = 60 * 1024 * 1024


def flip(value, bits, width):
    out = value
    for bit in range(width):
        if (bits >> bit) & 1:
            out = out + (1 << bit) * (1 - 2 * ((value // (1 << bit)) % 2))
    return out


FLOWS = {}
for _n in (0, 128):
    FLOWS |= {
        f"y{_n}": ("y", (0, 0), _n, 128, None),
        f"r{_n}": ("r", (0, 0), _n, 128, None),
        f"l{_n + 256}": ("l", (0, 0), _n + 256, 128, None),
    }
for _n in (0, 128):
    FLOWS |= {
        f"y{_n + 256}": ("y", (0, 0), _n + 256, 128, None),
        f"r{_n + 256}": ("r", (0, 0), _n + 256, 128, None),
        f"l{_n}": ("l", (0, 0), _n, 128, None),
    }
for _n in (0, 128):
    FLOWS |= {
        f"rr{_n}": ("r", (-1, 0), _n, 128, f"r{_n}"),
        f"ll{_n + 256}": ("l", (1, 0), _n + 256, 128, f"l{_n + 256}"),
        f"yr{_n}": ("r", (0, 1), _n, 128, f"y{_n}"),
        f"yl{_n}": ("l", (0, 1), _n, 128, f"y{_n}"),
        f"ly{_n}": ("y", (1, 0), _n + 256, 128, f"l{_n + 256}"),
        f"ry{_n}": ("y", (-1, 0), _n + 256, 128, f"r{_n + 256}"),
        f"lly{_n}": ("y", (2, 0), _n + 256, 128, f"ll{_n + 256}"),
    }
FLOWS |= {
    "yrr": ("r", (-1, 1), 0, 128, "yr0"),
    "yll": ("l", (1, 1), 128, 128, "yl128"),
}
NAMES = tuple(FLOWS)
PLACES = ((0, 0), (0, 1), (1, 0), (-1, 0), (2, 0), (1, 1), (-1, 1), (2, 1))


def landed(name):
    hop, (ox, oy), *_ = FLOWS[name]
    ox, oy = {"r": (ox - 1, oy), "l": (ox + 1, oy), "y": (ox, 1 - oy)}.get(hop, (ox, oy))
    return (2 if ox == -2 else ox), oy


def tower_kernel(
    fetch, slab, query, pos, lists, counts, item_counts, w_in, b_in, w_out,
    queries_out, meta_all, wanted, neg_log, cand,
    queries, chunk, table, rowbuf, staged, arrived, meta, w_in_v, w_out_v, logt,
    slab_sem, w_sem, own_sem, meta_send, meta_recv, a2a_send, a2a_recv, flow_send, flow_recv, core_send, core_recv, out_sem,
):
    t = lax.axis_index("catalog")
    x = lax.axis_index("query")
    d = lax.axis_index("dp")
    core = t % 2
    j = x * ND + d

    own_query = pltpu.make_async_copy(query, queries.at[j], own_sem.at[0])
    n_chunks = ROWS // SLAB_CHUNK
    depth = chunk.shape[0]

    def slab_copy(n):
        slot = n % depth
        rows = pl.ds(pl.multiple_of(n * SLAB_CHUNK, SLAB_CHUNK), SLAB_CHUNK)
        return pltpu.make_async_copy(slab.at[rows], chunk.at[slot], slab_sem.at[slot])

    for n in range(depth):
        slab_copy(n).start()

    own_query.start()

    meta_peers = [(dx, dd) for dx in range(NX) for dd in range(ND) if (dx, dd) != (0, 0)]
    right, left = (x + 1) % NX, (x + NX - 1) % NX
    hop_to = {
        "r": {"catalog": t, "query": right, "dp": d},
        "l": {"catalog": t, "query": left, "dp": d},
        "y": {"catalog": flip(t, 8, 4), "query": x, "dp": 1 - d},
    }
    sibling = {"catalog": flip(t, 1, 4), "query": x, "dp": d}

    barrier = pltpu.get_barrier_semaphore()
    n_peers = 0
    for k in range(1, NC):
        pl.semaphore_signal(barrier, inc=1, device_id={"catalog": flip(t, k, 4), "query": x, "dp": d}, device_id_type=MESH)
        n_peers += 1
    for dx, dd in meta_peers:
        pl.semaphore_signal(
            barrier, inc=1, device_id={"catalog": t, "query": (x + dx) % NX, "dp": (d + dd) % ND}, device_id_type=MESH
        )
        n_peers += 1
    pl.semaphore_signal(barrier, inc=1, device_id=hop_to["y"], device_id_type=MESH)
    n_peers += 1

    square = (QB, LIST)
    diagonal = lax.broadcasted_iota(jnp.int32, square, 0) == lax.broadcasted_iota(jnp.int32, square, 1)
    count = jnp.sum(jnp.where(diagonal, jnp.broadcast_to(counts[...], square), 0), axis=1, keepdims=True)
    listed = jnp.where(lax.broadcasted_iota(jnp.int32, square, 1) < count, lists[:, 0, :], NONE)
    meta[...] = jnp.full_like(meta, NONE)
    meta[0:QB, :] = pos[...]
    meta[QB : 2 * QB, 0:LIST] = listed

    pl.semaphore_wait(barrier, n_peers)

    def origin(place):
        ox, oy = place
        xo = (x + ox + NX) % NX
        return xo * ND + (1 - d if oy else d)

    def flow_copy(name):
        hop, place, first, count, _ = FLOWS[name]
        jo = origin(place)
        rows = pl.ds(pl.multiple_of(core * HALF + first, 128), count)
        src = query.at[rows] if place == (0, 0) else queries.at[jo, rows]
        return pltpu.make_async_remote_copy(
            src_ref=src,
            dst_ref=queries.at[jo, rows],
            send_sem=flow_send.at[NAMES.index(name)],
            recv_sem=flow_recv.at[NAMES.index(name)],
            device_id=hop_to[hop],
            device_id_type=MESH,
        )

    def core_copy(name):
        _, _, first, count, _ = FLOWS[name]
        part = queries.at[origin(landed(name)), pl.ds(pl.multiple_of(core * HALF + first, 128), count)]
        return pltpu.make_async_remote_copy(
            src_ref=part,
            dst_ref=part,
            send_sem=core_send.at[NAMES.index(name)],
            recv_sem=core_recv.at[NAMES.index(name)],
            device_id=sibling,
            device_id_type=MESH,
        )

    received, sent = set(), set()

    def send_ready():
        for name, flow in FLOWS.items():
            if name not in sent and (flow[4] is None or flow[4] in received):
                sent.add(name)
                flow_copy(name).start()

    def advance(*names):
        for name in names:
            flow_copy(name).wait_recv()
            received.add(name)
            send_ready()
            core_copy(name).start()

    send_ready()

    def meta_copy(n):
        dx, dd = meta_peers[n]
        return pltpu.make_async_remote_copy(
            src_ref=meta,
            dst_ref=meta_all.at[j],
            send_sem=meta_send.at[n],
            recv_sem=meta_recv.at[n],
            device_id={"catalog": t, "query": (x + dx) % NX, "dp": (d + dd) % ND},
            device_id_type=MESH,
        )

    for n in range(len(meta_peers)):
        meta_copy(n).start()
    def widen(first, count):
        @pl.loop(first, first + count)
        def _(n):
            slot = n % depth
            slab_copy(n).wait()

            @pl.loop(0, SLAB_CHUNK // 64)
            def _(i):
                rows = pl.ds(pl.multiple_of(i * 64, 64), 64)
                to = pl.ds(pl.multiple_of(n * SLAB_CHUNK + i * 64, 64), 64)
                table[to, :] = chunk[slot, rows, :].astype(jnp.float32)

            @pl.when(n + depth < n_chunks)
            def _():
                slab_copy(n + depth).start()

    widen(0, n_chunks // 2)
    advance("y0", "r0", "l256")
    widen(n_chunks // 2, n_chunks // 2)
    w_in_copy = pltpu.make_async_copy(w_in, w_in_v, w_sem.at[0])
    w_out_copy = pltpu.make_async_copy(w_out, w_out_v, w_sem.at[1])
    w_in_copy.start()
    w_out_copy.start()

    def a2a_copy(k):
        to = flip(t, k, 4)
        return pltpu.make_async_remote_copy(
            src_ref=staged.at[k],
            dst_ref=arrived.at[t],
            send_sem=a2a_send.at[k],
            recv_sem=a2a_recv.at[k],
            device_id={"catalog": to, "query": x, "dp": d},
            device_id_type=MESH,
        )

    for k in range(NC - 1, -1, -1):
        to = flip(t, k, 4)

        @pl.loop(0, SUB // 16)
        def _(i):
            for u in range(16):
                row = fetch[0, to, i * 16 + u]
                rowbuf[pl.ds(i * 16 + u, 1), :] = table[pl.ds(row, 1), :]

        if k:
            staged[k] = rowbuf[...].astype(jnp.bfloat16)
        else:
            arrived[t] = rowbuf[...].astype(jnp.bfloat16)
        if k == 12:
            advance("y128", "r128", "l384")
        if k == 6:
            advance("r256", "l0", "y256")
        if k:
            a2a_copy(k).start()

    advance("rr0", "ll256", "yr0", "yl0", "r384", "l128", "y384")
    w_in_copy.wait()
    w_out_copy.wait()

    def tower(group):
        base = 4 * flip(t // 4, group, 2)
        for k in range(4 * group, 4 * group + 4):
            if k:
                a2a_copy(k).wait_recv()
        rows = arrived[pl.ds(base, 4)].reshape(4 * SUB, E)
        hidden = jnp.maximum(jnp.dot(rows, w_in_v[...], preferred_element_type=jnp.float32) + b_in[...], 0.0).astype(jnp.bfloat16)
        y = jnp.dot(hidden, w_out_v[...], preferred_element_type=jnp.float32)
        normed = y * lax.rsqrt(jnp.sum(y * y, axis=-1, keepdims=True) + 1e-06)
        cand[pl.ds(base, 4)] = normed.astype(jnp.bfloat16).reshape(4, SUB, E)

    logt[...] = jnp.transpose(-jnp.log(item_counts[...].astype(jnp.float32)))
    own = logt[pl.ds(pl.multiple_of(j * SUB, SUB), SUB), :]
    for o in range(NC):
        neg_log[o * SUB : (o + 1) * SUB, :] = jnp.broadcast_to(own[:, o : o + 1], (SUB, 128))

    for n in range(len(meta_peers)):
        meta_copy(n).wait_recv()
    meta_all[j] = meta[...]
    for jo in range(NJ):
        offset = meta_all[jo, 0:QB, :] - (t * (NC * 512) + j * SUB)
        here = (offset >= 0) & (offset < NC * 512) & ((offset & 511) < SUB)
        wanted[jo] = jnp.where(here, (offset >> 9) * SUB + (offset & 511), -1)

    def query_out(place):
        jo = origin(place)
        return pltpu.make_async_copy(queries.at[jo], queries_out.at[jo], out_sem.at[PLACES.index(place)])

    def ship(*places):
        for place in places:
            for name in NAMES:
                if landed(name) == place:
                    core_copy(name).wait_recv()
            query_out(place).start()

    own_query.wait()
    query_out((0, 0)).start()
    advance("ly0", "ry0", "rr128", "ll384")
    tower(0)
    ship((0, 1), (1, 0), (-1, 0))
    advance("yr128", "yl128")
    tower(1)
    ship((2, 0))
    advance("ly128", "ry128", "lly0")
    tower(2)
    ship((1, 1), (-1, 1))
    tower(3)
    advance("yrr", "yll", "lly128")
    ship((2, 1))
    assert len(received) == len(sent) == len(NAMES)

    for place in PLACES:
        query_out(place).wait()
    for k in range(1, NC):
        a2a_copy(k).wait_send()
    for name in NAMES:
        flow_copy(name).wait_send()
        core_copy(name).wait_send()
    for n in range(len(meta_peers)):
        meta_copy(n).wait_send()


def run_tower(fetch, slab, query, pos, lists, counts, item_counts, w_in, b_in, w_out):
    dma = pltpu.SemaphoreType.DMA
    bf16, f32, i32 = jnp.bfloat16, jnp.float32, jnp.int32
    return pl.pallas_call(
        tower_kernel,
        out_shape=(
            jax.ShapeDtypeStruct((NJ, QROWS, E), bf16),
            jax.ShapeDtypeStruct((NJ, 2 * QB, 128), i32),
            jax.ShapeDtypeStruct((NJ, QB, 128), i32),
            jax.ShapeDtypeStruct((NC * SUB, 128), f32),
            jax.ShapeDtypeStruct((NC, SUB, E), bf16),
        ),
        in_specs=[SMEM, ANY, ANY, VMEM, VMEM, VMEM, VMEM, ANY, VMEM, ANY],
        out_specs=(ANY, VMEM, VMEM, VMEM, VMEM),
        scratch_shapes=[
            pltpu.VMEM((NJ, QROWS, E), bf16),
            pltpu.VMEM((8, SLAB_CHUNK, E), bf16),
            pltpu.VMEM((ROWS, E), f32),
            pltpu.VMEM((SUB, E), f32),
            pltpu.VMEM((NC, SUB, E), bf16),
            pltpu.VMEM((NC, SUB, E), bf16),
            pltpu.VMEM((2 * QB, 128), i32),
            pltpu.VMEM((E, H), bf16),
            pltpu.VMEM((H, E), bf16),
            pltpu.VMEM((512, NC), f32),
            dma((8,)),
            dma((2,)),
            dma((1,)),
            dma((NJ - 1,)),
            dma((NJ - 1,)),
            dma((NC,)),
            dma((NC,)),
            dma((len(NAMES),)),
            dma((len(NAMES),)),
            dma((len(NAMES),)),
            dma((len(NAMES),)),
            dma((NJ,)),
        ],
        compiler_params=pltpu.CompilerParams(
            collective_id=0, has_side_effects=True, vmem_limit_bytes=VMEM_LIMIT
        ),
        cost_estimate=pl.CostEstimate(flops=4 * 1024 * E * H, bytes_accessed=32 << 20, transcendentals=0),
        name="tower",
    )(fetch, slab, query, pos, lists, counts, item_counts, w_in, b_in, w_out)


def score_kernel(
    queries, meta, wanted, neg_log, cand,
    stats, cand_out,
    q, jobs, top, total, positive, q_sem, sem,
):
    x = lax.axis_index("query")
    cand_store = pltpu.make_async_copy(cand, cand_out, sem.at[0])
    loads = [pltpu.make_async_copy(queries.at[n], q.at[n], q_sem.at[n]) for n in range(NJ)]
    for load in loads:
        load.start()
    cand_store.start()

    top[...] = jnp.full_like(top, LOW)
    total[...] = jnp.zeros_like(total)
    positive[...] = jnp.zeros_like(positive)

    def list_blocks(jo, n):
        for b in range(QB):
            for e in range(LIST):
                block = meta[jo, QB + b, e]
                jobs[n] = (jo * QB + b) * NC + (block >> 2)
                n = n + jnp.where((block & (NONE + 3)) == x, 1, 0)
        return n

    n_jobs = lax.fori_loop(0, NJ, list_blocks, jnp.int32(0))
    for u in range(JOBS):
        jobs[n_jobs + u] = NJ * QB * NC

    for load in loads:
        load.wait()
    row_ids = lax.broadcasted_iota(jnp.int32, (SUB, 128), 0)

    @pl.loop(0, (n_jobs + JOBS - 1) // JOBS)
    def _(step):
        found = []
        for u in range(JOBS):
            job = jobs[step * JOBS + u]
            b, o = job >> 4, job & (NC - 1)
            b_q = jnp.minimum(b, NJ * QB - 1)
            jo, b_j = b_q >> 3, b_q & (QB - 1)
            block = q[jo, pl.ds(pl.multiple_of(b_j * 128, 128), 128), :]
            scores = lax.dot_general(cand[o], block, (((1,), (1,)), ((), ())), preferred_element_type=jnp.float32)
            scores = scores + neg_log[pl.ds(pl.multiple_of(o * SUB, SUB), SUB), :]
            want = wanted[jo, pl.ds(b_j, 1), :] - o * SUB
            peak = jnp.max(scores, axis=0, keepdims=True)
            mass = jnp.sum(jnp.exp(scores - peak), axis=0, keepdims=True)
            match = jnp.sum(jnp.where(row_ids == want, scores, 0.0), axis=0, keepdims=True)
            found.append((b, peak, mass, match))
        for b, peak, mass, match in found:
            at = pl.ds(b, 1)
            old = top[at, :]
            new = jnp.maximum(old, peak)
            total[at, :] = total[at, :] * jnp.exp(old - new) + mass * jnp.exp(peak - new)
            positive[at, :] = positive[at, :] + match
            top[at, :] = new

    for n in range(NJ):
        stats[n, 0:QB, :] = top[n * QB : (n + 1) * QB, :]
        stats[n, QB : 2 * QB, :] = total[n * QB : (n + 1) * QB, :]
        stats[n, 2 * QB : 3 * QB, :] = positive[n * QB : (n + 1) * QB, :]
    cand_store.wait()


def run_score(queries, meta, wanted, neg_log, cand):
    return pl.pallas_call(
        score_kernel,
        out_shape=(
            jax.ShapeDtypeStruct((NJ, 3 * QB, 128), jnp.float32),
            jax.ShapeDtypeStruct((NC, SUB, E), jnp.bfloat16),
        ),
        in_specs=[ANY, SMEM, VMEM, VMEM, VMEM],
        out_specs=(VMEM, ANY),
        scratch_shapes=[
            pltpu.VMEM((NJ, QROWS, E), jnp.bfloat16),
            pltpu.SMEM((NJ * QB * LIST + 2 * JOBS,), jnp.int32),
            pltpu.VMEM((NJ * QB + 8, 128), jnp.float32),
            pltpu.VMEM((NJ * QB + 8, 128), jnp.float32),
            pltpu.VMEM((NJ * QB + 8, 128), jnp.float32),
            pltpu.SemaphoreType.DMA((NJ,)),
            pltpu.SemaphoreType.DMA((1,)),
        ],
        compiler_params=pltpu.CompilerParams(vmem_limit_bytes=VMEM_LIMIT),
        cost_estimate=pl.CostEstimate(flops=1 << 29, bytes_accessed=10 << 20, transcendentals=1 << 20),
        name="score",
    )(queries, meta, wanted, neg_log, cand)


def merged(parts):
    tops = [part[0] for part in parts]
    top = functools.reduce(jnp.maximum, tops)
    total = functools.reduce(jnp.add, [part[1] * jnp.exp(part[0] - top) for part in parts])
    positive = functools.reduce(jnp.add, [part[2] for part in parts])
    return top, total, positive


def thirds(ref, index):
    return tuple(ref[index, n * QB : (n + 1) * QB, :] for n in range(3))


def merge_kernel(stats, loss, by_group, part, by_catalog, send_a, recv_a, send_b, recv_b):
    t = lax.axis_index("catalog")
    x = lax.axis_index("query")
    d = lax.axis_index("dp")
    j = x * ND + d
    peers = [(dx, dd) for dx in range(NX) for dd in range(ND) if (dx, dd) != (0, 0)]

    def group_peer(n):
        dx, dd = peers[n]
        return (x + dx) % NX, (d + dd) % ND

    barrier = pltpu.get_barrier_semaphore()
    for n in range(NJ - 1):
        xp, dp = group_peer(n)
        pl.semaphore_signal(barrier, inc=1, device_id={"catalog": t, "query": xp, "dp": dp}, device_id_type=MESH)
    for k in range(1, NC):
        pl.semaphore_signal(barrier, inc=1, device_id={"catalog": flip(t, k, 4), "query": x, "dp": d}, device_id_type=MESH)
    pl.semaphore_wait(barrier, NJ - 1 + NC - 1)

    def group_copy(n):
        xp, dp = group_peer(n)
        return pltpu.make_async_remote_copy(
            src_ref=stats.at[xp * ND + dp],
            dst_ref=by_group.at[j],
            send_sem=send_a.at[n],
            recv_sem=recv_a.at[n],
            device_id={"catalog": t, "query": xp, "dp": dp},
            device_id_type=MESH,
        )

    for n in range(NJ - 1):
        group_copy(n).start()
    by_group[j] = stats[j]
    for n in range(NJ - 1):
        group_copy(n).wait_recv()
    for n, value in enumerate(merged([thirds(by_group, i) for i in range(NJ)])):
        part[n * QB : (n + 1) * QB, :] = value

    def catalog_copy(k):
        return pltpu.make_async_remote_copy(
            src_ref=part,
            dst_ref=by_catalog.at[t],
            send_sem=send_b.at[k],
            recv_sem=recv_b.at[k],
            device_id={"catalog": flip(t, k, 4), "query": x, "dp": d},
            device_id_type=MESH,
        )

    for k in range(NC - 1, 0, -1):
        catalog_copy(k).start()
    by_catalog[t] = part[...]
    for k in range(NC - 1, 0, -1):
        catalog_copy(k).wait_recv()
    top, total, positive = merged([thirds(by_catalog, i) for i in range(NC)])
    loss[...] = top + jnp.log(total) - positive
    for n in range(NJ - 1):
        group_copy(n).wait_send()
    for k in range(1, NC):
        catalog_copy(k).wait_send()


def run_merge(stats):
    dma = pltpu.SemaphoreType.DMA
    return pl.pallas_call(
        merge_kernel,
        out_shape=jax.ShapeDtypeStruct((QB, 128), jnp.float32),
        in_specs=[VMEM],
        out_specs=VMEM,
        scratch_shapes=[
            pltpu.VMEM((NJ, 3 * QB, 128), jnp.float32),
            pltpu.VMEM((3 * QB, 128), jnp.float32),
            pltpu.VMEM((NC, 3 * QB, 128), jnp.float32),
            dma((NJ - 1,)),
            dma((NJ - 1,)),
            dma((NC,)),
            dma((NC,)),
        ],
        compiler_params=pltpu.CompilerParams(collective_id=1, has_side_effects=True, vmem_limit_bytes=16 * 1024 * 1024),
        name="merge",
    )(stats)


def per_device(
    slab, fetch_rows, w_in, b_in, w_out, query_emb, item_counts, tile_blocks, tile_count, pos_idx
):
    queries, meta, wanted, neg_log, cand = run_tower(
        fetch_rows,
        slab,
        query_emb,
        pos_idx.reshape(QB, 128),
        tile_blocks,
        tile_count.reshape(1, QB),
        item_counts.reshape(NC, 512),
        w_in,
        b_in.reshape(1, H),
        w_out,
    )
    stats, cand = run_score(queries, meta, wanted, neg_log, cand)
    loss = run_merge(stats)
    return (cand[None], loss.reshape(QROWS))


def solution(mesh):
    in_specs = (
        P("catalog", None),
        P("catalog", None, ("query", "dp")),
        P(),
        P(),
        P(),
        P(("query", "dp"), None),
        P("catalog", None, None),
        P(("query", "dp"), "catalog", None),
        P(("query", "dp"), "catalog"),
        P(("query", "dp")),
    )
    out_specs = (P("catalog", None, ("query", "dp"), None), P(("query", "dp")))
    return jax.shard_map(
        per_device, mesh=mesh, in_specs=in_specs, out_specs=out_specs, check_vma=False
    )
```

```python
import functools

import jax
import jax.numpy as jnp
from jax import lax
from jax.experimental import pallas as pl
from jax.experimental.pallas import tpu as pltpu
from jax.sharding import PartitionSpec as P

MESH = pl.DeviceIdType.MESH
ANY = pl.BlockSpec(memory_space=pl.ANY)
VMEM = pl.BlockSpec(memory_space=pltpu.VMEM)
SMEM = pl.BlockSpec(memory_space=pltpu.SMEM)

E = 512
H = 2048
NC = 16
NX = 4
ND = 2
NJ = NX * ND
SUB = 64
LIST = 8
ROWS = 16384
QROWS = 1024
QB = QROWS // 128
HALF = QROWS // 2
SLAB_CHUNK = 1024
JOBS = 16
NONE = 256
LOW = -1e30
VMEM_LIMIT = 60 * 1024 * 1024


def flip(value, bits, width):
    out = value
    for bit in range(width):
        if (bits >> bit) & 1:
            out = out + (1 << bit) * (1 - 2 * ((value // (1 << bit)) % 2))
    return out


FLOWS = {}
for _n in (0, 128):
    FLOWS |= {
        f"y{_n}": ("y", (0, 0), _n, 128, None),
        f"r{_n}": ("r", (0, 0), _n, 128, None),
        f"l{_n + 256}": ("l", (0, 0), _n + 256, 128, None),
    }
for _n in (0, 128):
    FLOWS |= {
        f"r{_n + 256}": ("r", (0, 0), _n + 256, 128, None),
        f"l{_n}": ("l", (0, 0), _n, 128, None),
    }
for _n in (0, 128):
    FLOWS |= {
        f"rr{_n}": ("r", (-1, 0), _n, 128, f"r{_n}"),
        f"ll{_n + 256}": ("l", (1, 0), _n + 256, 128, f"l{_n + 256}"),
        f"yr{_n}": ("r", (0, 1), _n, 128, f"y{_n}"),
        f"yl{_n}": ("l", (0, 1), _n, 128, f"y{_n}"),
        f"ly{_n}": ("y", (1, 0), _n + 256, 128, f"l{_n + 256}"),
        f"ry{_n}": ("y", (-1, 0), _n + 256, 128, f"r{_n + 256}"),
        f"lly{_n}": ("y", (2, 0), _n + 256, 128, f"ll{_n + 256}"),
    }
FLOWS |= {
    "ys": ("y", (0, 0), "own", 128, None),
    "w": ("w", (0, 1), "other", 128, "ys"),
    "yrr": ("r", (-1, 1), 0, 128, "yr0"),
    "yll": ("l", (1, 1), 128, 128, "yl128"),
}
NAMES = tuple(FLOWS)
PLACES = ((0, 0), (0, 1), (1, 0), (-1, 0), (2, 0), (1, 1), (-1, 1), (2, 1))


def landed(name):
    hop, (ox, oy), *_ = FLOWS[name]
    ox, oy = {"r": (ox - 1, oy), "l": (ox + 1, oy), "y": (ox, 1 - oy)}.get(hop, (ox, oy))
    return (2 if ox == -2 else ox), oy


def tower_kernel(
    fetch, slab, query, pos, lists, counts, item_counts, w_in, b_in, w_out,
    queries_out, meta_all, wanted, neg_log, cand,
    queries, chunk, table, rowbuf, staged, arrived, meta, w_in_v, w_out_v, logt,
    slab_sem, w_sem, own_sem, meta_send, meta_recv, a2a_send, a2a_recv, flow_send, flow_recv, core_send, core_recv, out_sem,
):
    t = lax.axis_index("catalog")
    x = lax.axis_index("query")
    d = lax.axis_index("dp")
    core = t % 2
    j = x * ND + d

    own_query = pltpu.make_async_copy(query, queries.at[j], own_sem.at[0])
    n_chunks = ROWS // SLAB_CHUNK
    depth = chunk.shape[0]

    def slab_copy(n):
        slot = n % depth
        rows = pl.ds(pl.multiple_of(n * SLAB_CHUNK, SLAB_CHUNK), SLAB_CHUNK)
        return pltpu.make_async_copy(slab.at[rows], chunk.at[slot], slab_sem.at[slot])

    for n in range(depth):
        slab_copy(n).start()

    own_query.start()

    meta_peers = [(dx, dd) for dx in range(NX) for dd in range(ND) if (dx, dd) != (0, 0)]
    right, left = (x + 1) % NX, (x + NX - 1) % NX
    hop_to = {
        "r": {"catalog": t, "query": right, "dp": d},
        "l": {"catalog": t, "query": left, "dp": d},
        "y": {"catalog": flip(t, 8, 4), "query": x, "dp": 1 - d},
        "w": {"catalog": flip(t, 8, 4), "query": x, "dp": d},
    }
    sibling = {"catalog": flip(t, 1, 4), "query": x, "dp": d}

    barrier = pltpu.get_barrier_semaphore()
    n_peers = 0
    for k in range(1, NC):
        pl.semaphore_signal(barrier, inc=1, device_id={"catalog": flip(t, k, 4), "query": x, "dp": d}, device_id_type=MESH)
        n_peers += 1
    for dx, dd in meta_peers:
        pl.semaphore_signal(
            barrier, inc=1, device_id={"catalog": t, "query": (x + dx) % NX, "dp": (d + dd) % ND}, device_id_type=MESH
        )
        n_peers += 1
    pl.semaphore_signal(barrier, inc=1, device_id=hop_to["y"], device_id_type=MESH)
    n_peers += 1

    square = (QB, LIST)
    diagonal = lax.broadcasted_iota(jnp.int32, square, 0) == lax.broadcasted_iota(jnp.int32, square, 1)
    count = jnp.sum(jnp.where(diagonal, jnp.broadcast_to(counts[...], square), 0), axis=1, keepdims=True)
    listed = jnp.where(lax.broadcasted_iota(jnp.int32, square, 1) < count, lists[:, 0, :], NONE)
    meta[...] = jnp.full_like(meta, NONE)
    meta[0:QB, :] = pos[...]
    meta[QB : 2 * QB, 0:LIST] = listed

    pl.semaphore_wait(barrier, n_peers)

    def origin(place):
        ox, oy = place
        xo = (x + ox + NX) % NX
        return xo * ND + (1 - d if oy else d)

    y_lo = t // 8

    def first_row(first):
        return {"own": 256 + 128 * y_lo, "other": 384 - 128 * y_lo}.get(first, first)

    def flow_copy(name):
        hop, place, first, count, _ = FLOWS[name]
        jo = origin(place)
        rows = pl.ds(pl.multiple_of(core * HALF + first_row(first), 128), count)
        src = query.at[rows] if place == (0, 0) else queries.at[jo, rows]
        return pltpu.make_async_remote_copy(
            src_ref=src,
            dst_ref=queries.at[jo, rows],
            send_sem=flow_send.at[NAMES.index(name)],
            recv_sem=flow_recv.at[NAMES.index(name)],
            device_id=hop_to[hop],
            device_id_type=MESH,
        )

    def core_copy(name):
        _, _, first, count, _ = FLOWS[name]
        first = first_row({"own": "other", "other": "own"}.get(first, first))
        part = queries.at[origin(landed(name)), pl.ds(pl.multiple_of(core * HALF + first, 128), count)]
        return pltpu.make_async_remote_copy(
            src_ref=part,
            dst_ref=part,
            send_sem=core_send.at[NAMES.index(name)],
            recv_sem=core_recv.at[NAMES.index(name)],
            device_id=sibling,
            device_id_type=MESH,
        )

    received, sent = set(), set()

    def send_ready():
        for name, flow in FLOWS.items():
            if name not in sent and (flow[4] is None or flow[4] in received):
                sent.add(name)
                flow_copy(name).start()

    def advance(*names):
        for name in names:
            flow_copy(name).wait_recv()
            received.add(name)
            send_ready()
            core_copy(name).start()

    send_ready()

    def meta_copy(n):
        dx, dd = meta_peers[n]
        return pltpu.make_async_remote_copy(
            src_ref=meta,
            dst_ref=meta_all.at[j],
            send_sem=meta_send.at[n],
            recv_sem=meta_recv.at[n],
            device_id={"catalog": t, "query": (x + dx) % NX, "dp": (d + dd) % ND},
            device_id_type=MESH,
        )

    for n in range(len(meta_peers)):
        meta_copy(n).start()
    def widen(first, count):
        @pl.loop(first, first + count)
        def _(n):
            slot = n % depth
            slab_copy(n).wait()

            @pl.loop(0, SLAB_CHUNK // 64)
            def _(i):
                rows = pl.ds(pl.multiple_of(i * 64, 64), 64)
                to = pl.ds(pl.multiple_of(n * SLAB_CHUNK + i * 64, 64), 64)
                table[to, :] = chunk[slot, rows, :].astype(jnp.float32)

            @pl.when(n + depth < n_chunks)
            def _():
                slab_copy(n + depth).start()

    widen(0, n_chunks // 2)
    advance("y0", "r0", "l256")
    widen(n_chunks // 2, n_chunks // 2)
    w_in_copy = pltpu.make_async_copy(w_in, w_in_v, w_sem.at[0])
    w_out_copy = pltpu.make_async_copy(w_out, w_out_v, w_sem.at[1])
    w_in_copy.start()
    w_out_copy.start()

    def a2a_copy(k):
        to = flip(t, k, 4)
        return pltpu.make_async_remote_copy(
            src_ref=staged.at[k],
            dst_ref=arrived.at[t],
            send_sem=a2a_send.at[k],
            recv_sem=a2a_recv.at[k],
            device_id={"catalog": to, "query": x, "dp": d},
            device_id_type=MESH,
        )

    for k in range(NC - 1, -1, -1):
        to = flip(t, k, 4)

        @pl.loop(0, SUB // 16)
        def _(i):
            for u in range(16):
                row = fetch[0, to, i * 16 + u]
                rowbuf[pl.ds(i * 16 + u, 1), :] = table[pl.ds(row, 1), :]

        if k:
            staged[k] = rowbuf[...].astype(jnp.bfloat16)
        else:
            arrived[t] = rowbuf[...].astype(jnp.bfloat16)
        if k == 12:
            advance("y128", "r128", "l384")
        if k == 6:
            advance("r256", "l0", "ys")
        if k:
            a2a_copy(k).start()

    advance("rr0", "ll256", "yr0", "yl0", "r384", "l128", "w")
    w_in_copy.wait()
    w_out_copy.wait()

    def tower(group):
        base = 4 * flip(t // 4, group, 2)
        for k in range(4 * group, 4 * group + 4):
            if k:
                a2a_copy(k).wait_recv()
        rows = arrived[pl.ds(base, 4)].reshape(4 * SUB, E)
        hidden = jnp.maximum(jnp.dot(rows, w_in_v[...], preferred_element_type=jnp.float32) + b_in[...], 0.0).astype(jnp.bfloat16)
        y = jnp.dot(hidden, w_out_v[...], preferred_element_type=jnp.float32)
        normed = y * lax.rsqrt(jnp.sum(y * y, axis=-1, keepdims=True) + 1e-06)
        cand[pl.ds(base, 4)] = normed.astype(jnp.bfloat16).reshape(4, SUB, E)

    logt[...] = jnp.transpose(-jnp.log(item_counts[...].astype(jnp.float32)))
    own = logt[pl.ds(pl.multiple_of(j * SUB, SUB), SUB), :]
    for o in range(NC):
        neg_log[o * SUB : (o + 1) * SUB, :] = jnp.broadcast_to(own[:, o : o + 1], (SUB, 128))

    for n in range(len(meta_peers)):
        meta_copy(n).wait_recv()
    meta_all[j] = meta[...]
    for jo in range(NJ):
        offset = meta_all[jo, 0:QB, :] - (t * (NC * 512) + j * SUB)
        here = (offset >= 0) & (offset < NC * 512) & ((offset & 511) < SUB)
        wanted[jo] = jnp.where(here, (offset >> 9) * SUB + (offset & 511), -1)

    def query_out(place):
        jo = origin(place)
        return pltpu.make_async_copy(queries.at[jo], queries_out.at[jo], out_sem.at[PLACES.index(place)])

    def ship(*places):
        for place in places:
            for name in NAMES:
                if landed(name) == place:
                    core_copy(name).wait_recv()
            query_out(place).start()

    own_query.wait()
    query_out((0, 0)).start()
    advance("ly0", "ry0", "rr128", "ll384")
    tower(0)
    ship((0, 1), (1, 0), (-1, 0))
    advance("yr128", "yl128")
    tower(1)
    ship((2, 0))
    advance("ly128", "ry128", "lly0")
    tower(2)
    ship((1, 1), (-1, 1))
    tower(3)
    advance("yrr", "yll", "lly128")
    ship((2, 1))
    assert len(received) == len(sent) == len(NAMES)

    for place in PLACES:
        query_out(place).wait()
    for k in range(1, NC):
        a2a_copy(k).wait_send()
    for name in NAMES:
        flow_copy(name).wait_send()
        core_copy(name).wait_send()
    for n in range(len(meta_peers)):
        meta_copy(n).wait_send()


def run_tower(fetch, slab, query, pos, lists, counts, item_counts, w_in, b_in, w_out):
    dma = pltpu.SemaphoreType.DMA
    bf16, f32, i32 = jnp.bfloat16, jnp.float32, jnp.int32
    return pl.pallas_call(
        tower_kernel,
        out_shape=(
            jax.ShapeDtypeStruct((NJ, QROWS, E), bf16),
            jax.ShapeDtypeStruct((NJ, 2 * QB, 128), i32),
            jax.ShapeDtypeStruct((NJ, QB, 128), i32),
            jax.ShapeDtypeStruct((NC * SUB, 128), f32),
            jax.ShapeDtypeStruct((NC, SUB, E), bf16),
        ),
        in_specs=[SMEM, ANY, ANY, VMEM, VMEM, VMEM, VMEM, ANY, VMEM, ANY],
        out_specs=(ANY, VMEM, VMEM, VMEM, VMEM),
        scratch_shapes=[
            pltpu.VMEM((NJ, QROWS, E), bf16),
            pltpu.VMEM((8, SLAB_CHUNK, E), bf16),
            pltpu.VMEM((ROWS, E), f32),
            pltpu.VMEM((SUB, E), f32),
            pltpu.VMEM((NC, SUB, E), bf16),
            pltpu.VMEM((NC, SUB, E), bf16),
            pltpu.VMEM((2 * QB, 128), i32),
            pltpu.VMEM((E, H), bf16),
            pltpu.VMEM((H, E), bf16),
            pltpu.VMEM((512, NC), f32),
            dma((8,)),
            dma((2,)),
            dma((1,)),
            dma((NJ - 1,)),
            dma((NJ - 1,)),
            dma((NC,)),
            dma((NC,)),
            dma((len(NAMES),)),
            dma((len(NAMES),)),
            dma((len(NAMES),)),
            dma((len(NAMES),)),
            dma((NJ,)),
        ],
        compiler_params=pltpu.CompilerParams(
            collective_id=0, has_side_effects=True, vmem_limit_bytes=VMEM_LIMIT
        ),
        cost_estimate=pl.CostEstimate(flops=4 * 1024 * E * H, bytes_accessed=32 << 20, transcendentals=0),
        name="tower",
    )(fetch, slab, query, pos, lists, counts, item_counts, w_in, b_in, w_out)


def score_kernel(
    queries, meta, wanted, neg_log, cand,
    stats, cand_out,
    q, jobs, top, total, positive, q_sem, sem,
):
    x = lax.axis_index("query")
    cand_store = pltpu.make_async_copy(cand, cand_out, sem.at[0])
    loads = [pltpu.make_async_copy(queries.at[n], q.at[n], q_sem.at[n]) for n in range(NJ)]
    for load in loads:
        load.start()
    cand_store.start()

    top[...] = jnp.full_like(top, LOW)
    total[...] = jnp.zeros_like(total)
    positive[...] = jnp.zeros_like(positive)

    def list_blocks(jo, n):
        for b in range(QB):
            for e in range(LIST):
                block = meta[jo, QB + b, e]
                jobs[n] = (jo * QB + b) * NC + (block >> 2)
                n = n + jnp.where((block & (NONE + 3)) == x, 1, 0)
        return n

    n_jobs = lax.fori_loop(0, NJ, list_blocks, jnp.int32(0))
    for u in range(JOBS):
        jobs[n_jobs + u] = NJ * QB * NC

    for load in loads:
        load.wait()
    row_ids = lax.broadcasted_iota(jnp.int32, (SUB, 128), 0)

    @pl.loop(0, (n_jobs + JOBS - 1) // JOBS)
    def _(step):
        found = []
        for u in range(JOBS):
            job = jobs[step * JOBS + u]
            b, o = job >> 4, job & (NC - 1)
            b_q = jnp.minimum(b, NJ * QB - 1)
            jo, b_j = b_q >> 3, b_q & (QB - 1)
            block = q[jo, pl.ds(pl.multiple_of(b_j * 128, 128), 128), :]
            scores = lax.dot_general(cand[o], block, (((1,), (1,)), ((), ())), preferred_element_type=jnp.float32)
            scores = scores + neg_log[pl.ds(pl.multiple_of(o * SUB, SUB), SUB), :]
            want = wanted[jo, pl.ds(b_j, 1), :] - o * SUB
            peak = jnp.max(scores, axis=0, keepdims=True)
            mass = jnp.sum(jnp.exp(scores - peak), axis=0, keepdims=True)
            match = jnp.sum(jnp.where(row_ids == want, scores, 0.0), axis=0, keepdims=True)
            found.append((b, peak, mass, match))
        for b, peak, mass, match in found:
            at = pl.ds(b, 1)
            old = top[at, :]
            new = jnp.maximum(old, peak)
            total[at, :] = total[at, :] * jnp.exp(old - new) + mass * jnp.exp(peak - new)
            positive[at, :] = positive[at, :] + match
            top[at, :] = new

    for n in range(NJ):
        stats[n, 0:QB, :] = top[n * QB : (n + 1) * QB, :]
        stats[n, QB : 2 * QB, :] = total[n * QB : (n + 1) * QB, :]
        stats[n, 2 * QB : 3 * QB, :] = positive[n * QB : (n + 1) * QB, :]
    cand_store.wait()


def run_score(queries, meta, wanted, neg_log, cand):
    return pl.pallas_call(
        score_kernel,
        out_shape=(
            jax.ShapeDtypeStruct((NJ, 3 * QB, 128), jnp.float32),
            jax.ShapeDtypeStruct((NC, SUB, E), jnp.bfloat16),
        ),
        in_specs=[ANY, SMEM, VMEM, VMEM, VMEM],
        out_specs=(VMEM, ANY),
        scratch_shapes=[
            pltpu.VMEM((NJ, QROWS, E), jnp.bfloat16),
            pltpu.SMEM((NJ * QB * LIST + 2 * JOBS,), jnp.int32),
            pltpu.VMEM((NJ * QB + 8, 128), jnp.float32),
            pltpu.VMEM((NJ * QB + 8, 128), jnp.float32),
            pltpu.VMEM((NJ * QB + 8, 128), jnp.float32),
            pltpu.SemaphoreType.DMA((NJ,)),
            pltpu.SemaphoreType.DMA((1,)),
        ],
        compiler_params=pltpu.CompilerParams(vmem_limit_bytes=VMEM_LIMIT),
        cost_estimate=pl.CostEstimate(flops=1 << 29, bytes_accessed=10 << 20, transcendentals=1 << 20),
        name="score",
    )(queries, meta, wanted, neg_log, cand)


def merged(parts):
    tops = [part[0] for part in parts]
    top = functools.reduce(jnp.maximum, tops)
    total = functools.reduce(jnp.add, [part[1] * jnp.exp(part[0] - top) for part in parts])
    positive = functools.reduce(jnp.add, [part[2] for part in parts])
    return top, total, positive


def thirds(ref, index):
    return tuple(ref[index, n * QB : (n + 1) * QB, :] for n in range(3))


def merge_kernel(stats, loss, by_group, part, by_catalog, send_a, recv_a, send_b, recv_b):
    t = lax.axis_index("catalog")
    x = lax.axis_index("query")
    d = lax.axis_index("dp")
    j = x * ND + d
    peers = [(dx, dd) for dx in range(NX) for dd in range(ND) if (dx, dd) != (0, 0)]

    def group_peer(n):
        dx, dd = peers[n]
        return (x + dx) % NX, (d + dd) % ND

    barrier = pltpu.get_barrier_semaphore()
    for n in range(NJ - 1):
        xp, dp = group_peer(n)
        pl.semaphore_signal(barrier, inc=1, device_id={"catalog": t, "query": xp, "dp": dp}, device_id_type=MESH)
    for k in range(1, NC):
        pl.semaphore_signal(barrier, inc=1, device_id={"catalog": flip(t, k, 4), "query": x, "dp": d}, device_id_type=MESH)
    pl.semaphore_wait(barrier, NJ - 1 + NC - 1)

    def group_copy(n):
        xp, dp = group_peer(n)
        return pltpu.make_async_remote_copy(
            src_ref=stats.at[xp * ND + dp],
            dst_ref=by_group.at[j],
            send_sem=send_a.at[n],
            recv_sem=recv_a.at[n],
            device_id={"catalog": t, "query": xp, "dp": dp},
            device_id_type=MESH,
        )

    for n in range(NJ - 1):
        group_copy(n).start()
    by_group[j] = stats[j]
    for n in range(NJ - 1):
        group_copy(n).wait_recv()
    for n, value in enumerate(merged([thirds(by_group, i) for i in range(NJ)])):
        part[n * QB : (n + 1) * QB, :] = value

    def catalog_copy(k):
        return pltpu.make_async_remote_copy(
            src_ref=part,
            dst_ref=by_catalog.at[t],
            send_sem=send_b.at[k],
            recv_sem=recv_b.at[k],
            device_id={"catalog": flip(t, k, 4), "query": x, "dp": d},
            device_id_type=MESH,
        )

    for k in range(NC - 1, 0, -1):
        catalog_copy(k).start()
    by_catalog[t] = part[...]
    for k in range(NC - 1, 0, -1):
        catalog_copy(k).wait_recv()
    top, total, positive = merged([thirds(by_catalog, i) for i in range(NC)])
    loss[...] = top + jnp.log(total) - positive
    for n in range(NJ - 1):
        group_copy(n).wait_send()
    for k in range(1, NC):
        catalog_copy(k).wait_send()


def run_merge(stats):
    dma = pltpu.SemaphoreType.DMA
    return pl.pallas_call(
        merge_kernel,
        out_shape=jax.ShapeDtypeStruct((QB, 128), jnp.float32),
        in_specs=[VMEM],
        out_specs=VMEM,
        scratch_shapes=[
            pltpu.VMEM((NJ, 3 * QB, 128), jnp.float32),
            pltpu.VMEM((3 * QB, 128), jnp.float32),
            pltpu.VMEM((NC, 3 * QB, 128), jnp.float32),
            dma((NJ - 1,)),
            dma((NJ - 1,)),
            dma((NC,)),
            dma((NC,)),
        ],
        compiler_params=pltpu.CompilerParams(collective_id=1, has_side_effects=True, vmem_limit_bytes=16 * 1024 * 1024),
        name="merge",
    )(stats)


def per_device(
    slab, fetch_rows, w_in, b_in, w_out, query_emb, item_counts, tile_blocks, tile_count, pos_idx
):
    queries, meta, wanted, neg_log, cand = run_tower(
        fetch_rows,
        slab,
        query_emb,
        pos_idx.reshape(QB, 128),
        tile_blocks,
        tile_count.reshape(1, QB),
        item_counts.reshape(NC, 512),
        w_in,
        b_in.reshape(1, H),
        w_out,
    )
    stats, cand = run_score(queries, meta, wanted, neg_log, cand)
    loss = run_merge(stats)
    return (cand[None], loss.reshape(QROWS))


def solution(mesh):
    in_specs = (
        P("catalog", None),
        P("catalog", None, ("query", "dp")),
        P(),
        P(),
        P(),
        P(("query", "dp"), None),
        P("catalog", None, None),
        P(("query", "dp"), "catalog", None),
        P(("query", "dp"), "catalog"),
        P(("query", "dp")),
    )
    out_specs = (P("catalog", None, ("query", "dp"), None), P(("query", "dp")))
    return jax.shard_map(
        per_device, mesh=mesh, in_specs=in_specs, out_specs=out_specs, check_vma=False
    )
```
